128 devices in a mesh: row: 8 (over y, core), col: 16 (over z, x).
Axes of the slice: x: 4, y: 4, z: 4, core: 2. Of those that a mesh axis runs over, the one named last changes fastest.
Arguments:
- waveforms: bfloat16 [128, 3, 160, 1024], P(('row', 'col')), may hold values from -600 to 600, as said below
- availability: int32 [128, 2], P(('row', 'col')), may hold values from 0 to 160, as said below
- pair_slot: int32 [128, 128], replicated, may hold values from 0 to 16383, as said below
- old_stack: float32 [16384, 3, 3, 512], P(('row', 'col')), may hold values from -1.8 to 1.8
Outputs:
- new_stack: float32 [16384, 3, 3, 512], P(('row', 'col'))
The draws below stay inside these ranges and needn't reach their ends.
Inputs may be any that keep to these rules, and one draw needn't show every extreme that they name: waveforms[s, c, g, n] lies in the stated range. Station s has data in segments availability[s, 0] to availability[s, 1] - 1, with availability[s, 0] < 80 < availability[s, 1]. pair_slot holds every number of 0 .. 16383 once; its owner is pair_slot // 128. Pair a, b belongs to tile (a // 16) * 16 + b % 16. At most 2 pairs of one tile have one owner, and some tile and owner reach it; the number of pairs of tile d with owner o depends only on (o - d) modulo 128.
All inputs are finite; a program needn't handle non-finite values.
Results may differ from the reference program's by a relative error of at most 0.008.
Values may be sent and summed in bfloat16 or wider, within the bound.
No kernel may reach another device: no remote copies, remote signals or barrier semaphores. Data moves between devices by JAX's collectives and lax.ppermute only.
A program may use at most 256 MiB of HBM per device.

```python
import math
import jax
import jax.numpy as jnp
from jax import lax

ST_DEV = 1
SEGMENTS = 160
COMPONENTS = 3
SAMPLES = 1024
LAG_BINS = 512
BAND_HALF = 64
FREQ_BINS = 512
STATIONS = 128
PAIRS = 16384
N_ROW = 8
N_COL = 16


def draw_waveforms(key, part):
    key = jax.random.fold_in(key, 11)
    keys = jax.random.split(key, 3)
    shape = (STATIONS, COMPONENTS, SEGMENTS, SAMPLES)
    white = jax.random.truncated_normal(keys[0], -4.0, 4.0, shape, jnp.float32)
    gains = jnp.exp(jax.random.uniform(keys[1], (STATIONS, COMPONENTS, 1, 1), jnp.float32, 0.0, math.log(10.0)))
    sample_ids = jnp.arange(SAMPLES, dtype=jnp.int32)
    signal = white
    for tone in range(2):
        tone_key = jax.random.fold_in(keys[2], tone)
        bin_key, amp_key, phase_key = jax.random.split(tone_key, 3)
        tone_bins = jax.random.randint(bin_key, (STATIONS, COMPONENTS, 1, 1), 1, FREQ_BINS)
        amplitude = jnp.exp(jax.random.uniform(amp_key, (STATIONS, COMPONENTS, 1, 1), jnp.float32, math.log(2.0), math.log(8.0)))
        phases = jax.random.uniform(phase_key, (STATIONS, COMPONENTS, SEGMENTS, 1), jnp.float32, -math.pi, math.pi)
        turns = (tone_bins * sample_ids % SAMPLES).astype(jnp.float32) * (2.0 * math.pi / SAMPLES)
        signal = signal + amplitude * jnp.sin(turns + phases)
    return (gains * signal).astype(jnp.bfloat16)


def draw_availability(key, part):
    key = jax.random.fold_in(key, 13)
    first_key, last_key = jax.random.split(key, 2)
    first_seg = jax.random.randint(first_key, (STATIONS,), 0, SEGMENTS // 2)
    end_seg = jax.random.randint(last_key, (STATIONS,), SEGMENTS // 2 + 1, SEGMENTS + 1)
    return jnp.stack([first_seg, end_seg], axis=1).astype(jnp.int32)


def draw_pair_slot(key, part):
    key = jax.random.fold_in(key, 17)
    key_count, key_order, key_slot = jax.random.split(key, 3)
    devices = N_ROW * N_COL
    share = ST_DEV * ST_DEV
    per_owner = share * devices
    row_block = ST_DEV * N_COL
    quarter = devices // 4
    pattern = jnp.concatenate([jnp.full((quarter,), 2 * share, jnp.int32), jnp.full((devices - 2 * quarter,), share, jnp.int32), jnp.zeros((quarter,), jnp.int32)])
    counts = jax.random.permutation(key_count, pattern)
    run_ends = jnp.cumsum(counts).astype(jnp.int32)
    position = jnp.arange(per_owner, dtype=jnp.int32)
    offset_of = jnp.sum((run_ends[None, :] <= position[:, None]).astype(jnp.int32), axis=1)
    rank_of = position - (run_ends - counts)[offset_of]
    scores = jax.random.randint(key_order, (devices, per_owner), 0, 2 ** 30 // per_owner) * per_owner + position[None, :]
    order = jnp.argsort(scores, axis=1, stable=True)
    tile_ids = jnp.arange(devices, dtype=jnp.int32)[:, None]
    owner_ids = (tile_ids + offset_of[order]) % devices
    grid = (jnp.arange(devices, dtype=jnp.int32)[:, None] - jnp.arange(devices, dtype=jnp.int32)[None, :]) % devices
    matrix = counts[grid]
    starts = jnp.cumsum(matrix, axis=1) - matrix
    slot_ids = starts[owner_ids, tile_ids] + rank_of[order]
    shuffle = jax.random.permutation(key_slot, per_owner).astype(jnp.int32)
    values = owner_ids * per_owner + shuffle[slot_ids]
    values = values.reshape(N_ROW, N_COL, row_block, N_ROW, ST_DEV)
    return jnp.transpose(values, (0, 2, 3, 1, 4)).reshape(STATIONS, STATIONS).astype(jnp.int32)


def shard_levels(rng, dims, shards, low, largest):
    def one(dim, shards_of):
        steps = jax.random.uniform(jax.random.fold_in(jax.random.fold_in(rng, 6), dim), (shards_of,), jnp.float32, low / len(shards), largest / len(shards))
        return jnp.repeat(jnp.exp(steps), dims[dim] // shards_of).reshape((-1,) + (1,) * (len(dims) - dim - 1))

    level = one(*shards[0])
    for cut in shards[1:]:
        level = level * one(*cut)
    return level


def noise(rng, dims, scale, bound, cuts=(), kind=jnp.bfloat16):
    values = scale * jax.random.normal(rng, dims, jnp.float32)
    if cuts:
        values = values * shard_levels(rng, dims, cuts, -0.22, 0.18)
    return jnp.clip(values, -bound, bound).astype(kind)


def setup_inputs(seed: int = 0) -> dict:
    seeds = jax.random.split(jax.random.key(seed), 5)
    waveforms = draw_waveforms(jax.random.fold_in(seeds[4], 71), 0)
    availability = draw_availability(jax.random.fold_in(seeds[4], 71), 0)
    pair_slot = draw_pair_slot(jax.random.fold_in(seeds[4], 71), 0)
    old_stack = noise(seeds[3], (PAIRS, COMPONENTS, COMPONENTS, LAG_BINS), 0.3, 1.8, ((0, 128),), jnp.float32)
    return dict(waveforms=waveforms, availability=availability, pair_slot=pair_slot, old_stack=old_stack)


EPSILON = 1e-06

def dft_table():
    sample_ids = jnp.arange(SAMPLES, dtype=jnp.int32)
    bin_ids = jnp.arange(FREQ_BINS, dtype=jnp.int32)
    turns = (sample_ids[:, None] * bin_ids[None, :] % SAMPLES).astype(jnp.float32) * (2.0 * math.pi / SAMPLES)
    return jnp.concatenate([jnp.cos(turns), -jnp.sin(turns)], axis=1).astype(jnp.bfloat16)

def band_table():
    bin_ids = jnp.arange(FREQ_BINS, dtype=jnp.int32)
    near_bins = (jnp.abs(bin_ids[:, None] - bin_ids[None, :]) <= BAND_HALF).astype(jnp.float32)
    return near_bins / lax.optimization_barrier(jnp.sum(near_bins, axis=0, keepdims=True))

def lag_table():
    bin_ids = jnp.arange(FREQ_BINS, dtype=jnp.int32)
    lag_ids = jnp.arange(LAG_BINS, dtype=jnp.int32) - LAG_BINS // 2
    turns = (bin_ids[:, None] * lag_ids[None, :] % SAMPLES).astype(jnp.float32) * (2.0 * math.pi / SAMPLES)
    weight = jnp.where(bin_ids == 0, 1.0, 2.0).astype(jnp.float32) / math.sqrt(FREQ_BINS)
    return jnp.concatenate([weight[:, None] * jnp.cos(turns), -weight[:, None] * jnp.sin(turns)], axis=0).astype(jnp.bfloat16)

def segment_mask(availability):
    segment_ids = jnp.arange(SEGMENTS, dtype=jnp.int32)
    inside = (segment_ids[None, :] >= availability[:, 0:1]) & (segment_ids[None, :] < availability[:, 1:2])
    return inside.astype(jnp.float32)

def whiten(waveforms, mask):
    station_count = waveforms.shape[0]
    flat_waves = waveforms.reshape(-1, SAMPLES)
    spectrum = jnp.dot(flat_waves, dft_table(), preferred_element_type=jnp.float32)
    real_part = spectrum[:, :FREQ_BINS]
    imag_part = spectrum[:, FREQ_BINS:]
    smooth = jnp.dot(real_part * real_part + imag_part * imag_part, band_table(), precision=lax.Precision.HIGHEST)
    factor = lax.rsqrt(smooth + EPSILON).reshape(station_count, COMPONENTS, SEGMENTS, 1, FREQ_BINS)
    factor = factor * mask[:, None, :, None, None]
    shaped = spectrum.reshape(station_count, COMPONENTS, SEGMENTS, 2, FREQ_BINS) * factor
    return jnp.transpose(shaped, (0, 1, 3, 2, 4)).astype(jnp.bfloat16)

def tile_partial(row_panel, row_mask, col_panel, col_mask, row_ids, col_ids):
    row_count = row_panel.shape[0]
    col_count = col_panel.shape[0]
    folded = row_panel.reshape(row_count, COMPONENTS, 2 * SEGMENTS, FREQ_BINS).astype(jnp.float32)
    turned = jnp.concatenate([row_panel[:, :, 1], -row_panel[:, :, 0]], axis=2)
    turned = turned.reshape(row_count, COMPONENTS, 2 * SEGMENTS, FREQ_BINS).astype(jnp.float32)
    col_folded = col_panel.reshape(col_count, COMPONENTS, 2 * SEGMENTS, FREQ_BINS).astype(jnp.float32)
    real_cross = jnp.einsum('ackf,bdkf->bacdf', folded, col_folded)
    imag_cross = jnp.einsum('ackf,bdkf->bacdf', turned, col_folded)
    cross_spec = jnp.concatenate([real_cross, imag_cross], axis=4).astype(jnp.bfloat16)
    lagged = jnp.dot(cross_spec.reshape(-1, 2 * FREQ_BINS), lag_table(), preferred_element_type=jnp.float32)
    lagged = lagged.reshape(col_count, row_count, COMPONENTS * COMPONENTS * LAG_BINS)
    counts = jnp.dot(col_mask, row_mask.T, precision=lax.Precision.HIGHEST)
    keep_pair = (col_ids[:, None] != row_ids[None, :]).astype(jnp.float32)
    return lagged * (keep_pair / counts)[:, :, None]

def reference(waveforms, availability, pair_slot, old_stack):
    masks = segment_mask(availability)
    panels = whiten(waveforms, masks)
    row_size = ST_DEV * N_COL
    station_count = waveforms.shape[0]
    row_width = COMPONENTS * COMPONENTS * LAG_BINS
    all_ids = jnp.arange(station_count, dtype=jnp.int32)

    def one_block(block_index, stack_rows):
        begin_at = (block_index * row_size).astype(jnp.int32)
        row_panel = lax.dynamic_slice_in_dim(panels, begin_at, row_size, 0)
        row_mask = lax.dynamic_slice_in_dim(masks, begin_at, row_size, 0)
        row_ids = begin_at + jnp.arange(row_size, dtype=jnp.int32)
        tile_rows = tile_partial(row_panel, row_mask, panels, masks, row_ids, all_ids)
        slot_rows = lax.dynamic_slice_in_dim(pair_slot, begin_at, row_size, 0).T
        return stack_rows.at[slot_rows.reshape(-1)].add(tile_rows.reshape(-1, row_width))
    stack_rows = lax.fori_loop(0, station_count // row_size, one_block, old_stack.reshape(-1, row_width))
    return stack_rows.reshape(old_stack.shape)
```

```python
import functools
import math

import jax
import jax.numpy as jnp
import ml_dtypes
import numpy as np
from jax import lax
from jax.experimental import pallas as pl
from jax.experimental.pallas import tpu as pltpu
from jax.sharding import PartitionSpec as P

SEGMENTS = 160
COMPONENTS = 3
SAMPLES = 1024
LAG_BINS = 512
BAND_HALF = 64
FREQ_BINS = 512
DEVICES = 128
STATIONS = 128
PER_OWNER = 128
BINS = FREQ_BINS // DEVICES
PARTS = 2 * BINS
LANES = COMPONENTS * SEGMENTS
LANES_FULL = 512
PRODUCTS = COMPONENTS * COMPONENTS
VALUES = PRODUCTS * PARTS

EPSILON = 1e-06
VMEM_LIMIT = 56 * 1024 * 1024
NT = (((1,), (1,)), ((), ()))
TN = (((0,), (0,)), ((), ()))


def dft_table():
    turns = np.arange(FREQ_BINS)[:, None] * np.arange(SAMPLES)[None, :] % SAMPLES
    turns = turns.astype(np.float32) * np.float32(2.0 * math.pi / SAMPLES)
    table = np.concatenate([np.cos(turns), -np.sin(turns)], axis=0)
    return table.astype(ml_dtypes.bfloat16)


def band_tables():
    bin_ids = np.arange(FREQ_BINS)
    near = np.abs(bin_ids[:, None] - bin_ids[None, :]) <= BAND_HALF
    return near.astype(ml_dtypes.bfloat16), (1.0 / near.sum(axis=1, keepdims=True)).astype(np.float32)


def lag_table():
    bin_ids = np.arange(FREQ_BINS)
    lag_ids = np.arange(LAG_BINS) - LAG_BINS // 2
    turns = bin_ids[:, None] * lag_ids[None, :] % SAMPLES
    turns = turns.astype(np.float32) * np.float32(2.0 * math.pi / SAMPLES)
    weight = np.where(bin_ids == 0, 1.0, 2.0).astype(np.float32)[:, None] / np.float32(math.sqrt(FREQ_BINS))
    both = np.stack([weight * np.cos(turns), -weight * np.sin(turns)])
    both = both.reshape(2, DEVICES, BINS, LAG_BINS).transpose(1, 0, 2, 3)
    return both.reshape(2 * FREQ_BINS, LAG_BINS).astype(ml_dtypes.bfloat16)


def whiten_kernel(avail_ref, wave_ref, dft_ref, band_ref, share_ref, out_ref, wave_full):
    wave_full[:LANES] = wave_ref[...]
    wave_full[LANES:] = jnp.zeros((LANES_FULL - LANES, SAMPLES), jnp.bfloat16)
    waves = wave_full[...]
    real = lax.dot_general(dft_ref[:FREQ_BINS], waves, NT, preferred_element_type=jnp.float32)
    imag = lax.dot_general(dft_ref[FREQ_BINS:], waves, NT, preferred_element_type=jnp.float32)
    power = real * real + imag * imag
    high = power.astype(jnp.bfloat16)
    low = (power - high.astype(jnp.float32)).astype(jnp.bfloat16)
    band = band_ref[...]
    smooth = jnp.dot(band, high, preferred_element_type=jnp.float32) + jnp.dot(
        band, low, preferred_element_type=jnp.float32
    )
    lane = lax.broadcasted_iota(jnp.int32, (1, LANES_FULL), 1)
    segment = lane % SEGMENTS
    first, last = avail_ref[0, 0], avail_ref[0, 1]
    mask = ((segment >= first) & (segment < last) & (lane < LANES)).astype(jnp.float32)
    factor = lax.rsqrt(smooth * share_ref[...] + EPSILON) * mask
    spare = jnp.where(lane == LANES, first, jnp.where(lane == LANES + 1, last, 0)).astype(jnp.float32)
    real = (real * factor + spare).reshape(FREQ_BINS // 8, 8, LANES_FULL)
    imag = (imag * factor + spare).reshape(FREQ_BINS // 8, 8, LANES_FULL)
    lower = lax.broadcasted_iota(jnp.int32, (1, 8, 1), 1) < BINS
    out_ref[:, 0] = jnp.where(lower, real, pltpu.roll(imag, BINS, 1)).astype(jnp.bfloat16)
    out_ref[:, 1] = jnp.where(lower, pltpu.roll(real, BINS, 1), imag).astype(jnp.bfloat16)


def whiten(waves, availability):
    near, share = band_tables()
    out = pl.pallas_call(
        whiten_kernel,
        out_shape=jax.ShapeDtypeStruct((FREQ_BINS // 8, 2, PARTS, LANES_FULL), jnp.bfloat16),
        in_specs=[pl.BlockSpec(memory_space=pltpu.SMEM)] + [pl.BlockSpec(memory_space=pltpu.VMEM)] * 4,
        out_specs=pl.BlockSpec(memory_space=pltpu.VMEM),
        scratch_shapes=[pltpu.VMEM((LANES_FULL, SAMPLES), jnp.bfloat16)],
        compiler_params=pltpu.CompilerParams(vmem_limit_bytes=VMEM_LIMIT),
    )(availability, waves, jnp.asarray(dft_table()), jnp.asarray(near), jnp.asarray(share))
    return out.reshape(DEVICES, PARTS, LANES_FULL)


def cross_kernel(slot_ref, spec_ref, out_ref, spec_full, planes, turned, placed):
    wide = spec_ref[...].astype(jnp.float32).reshape(STATIONS * PARTS, LANES_FULL)
    tiles = LANES_FULL // 128
    for t in range(tiles):
        spec_full[t] = wide[:, t * 128 : (t + 1) * 128]

    def part(row):
        return jnp.concatenate(
            [spec_full[t, pl.ds(row, STATIONS, stride=PARTS), :] for t in range(tiles)], axis=1
        )

    head = part(0)
    first = jnp.broadcast_to(head[:, LANES : LANES + 1], (STATIONS, STATIONS))
    last = jnp.broadcast_to(head[:, LANES + 1 : LANES + 2], (STATIONS, STATIONS))
    counts = jnp.minimum(last, last.T) - jnp.maximum(first, first.T)
    one = lax.broadcasted_iota(jnp.int32, (STATIONS, STATIONS), 0)
    two = lax.broadcasted_iota(jnp.int32, (STATIONS, STATIONS), 1)
    scale = jnp.where(one == two, 0.0, 1.0 / counts)

    def fold(values):
        return jnp.concatenate(
            [values[:, c * SEGMENTS : (c + 1) * SEGMENTS] for c in range(COMPONENTS)], axis=0
        ).astype(jnp.bfloat16)

    def product(x, y):
        return lax.dot_general(x, y, NT, preferred_element_type=jnp.float32)

    for f in range(BINS):
        real, imag = fold(part(f)), fold(part(BINS + f))
        both = (product(real, real) + product(imag, imag), product(imag, real) - product(real, imag))
        for p in range(2):
            for c in range(COMPONENTS):
                for d in range(COMPONENTS):
                    plane = both[p][c * STATIONS : (c + 1) * STATIONS, d * STATIONS : (d + 1) * STATIONS]
                    row = (c * COMPONENTS + d) * PARTS + p * BINS + f
                    planes[pl.ds(row, STATIONS, stride=VALUES), :] = plane * scale

    def place(a, carry):
        turned[:, :VALUES] = planes[pl.ds(a * VALUES, VALUES), :].T
        for b in range(STATIONS):
            placed[pl.ds(slot_ref[a * STATIONS + b], 1), :] = turned[b : b + 1, :]
        return carry

    lax.fori_loop(0, STATIONS, place, 0)

    def finish(owner, carry):
        out_ref[owner] = placed[pl.ds(owner * PER_OWNER, PER_OWNER), :].T[:VALUES].astype(jnp.bfloat16)
        return carry

    lax.fori_loop(0, DEVICES, finish, 0)


def cross(slots, spectra):
    return pl.pallas_call(
        cross_kernel,
        out_shape=jax.ShapeDtypeStruct((DEVICES, VALUES, PER_OWNER), jnp.bfloat16),
        in_specs=[pl.BlockSpec(memory_space=pltpu.SMEM), pl.BlockSpec(memory_space=pltpu.VMEM)],
        out_specs=pl.BlockSpec(memory_space=pltpu.VMEM),
        scratch_shapes=[
            pltpu.VMEM((LANES_FULL // 128, STATIONS * PARTS, 128), jnp.float32),
            pltpu.VMEM((STATIONS * VALUES, STATIONS), jnp.float32),
            pltpu.VMEM((STATIONS, 128), jnp.float32),
            pltpu.VMEM((DEVICES * PER_OWNER, 128), jnp.float32),
        ],
        compiler_params=pltpu.CompilerParams(vmem_limit_bytes=VMEM_LIMIT),
    )(slots, spectra)


def lag_kernel(cross_ref, table_ref, old_ref, out_ref):
    row = pl.multiple_of(pl.program_id(0) * PARTS, PARTS)
    spectra = cross_ref[:, pl.ds(row, PARTS), :].reshape(2 * FREQ_BINS, PER_OWNER)
    lagged = lax.dot_general(spectra, table_ref[...], TN, preferred_element_type=jnp.float32)
    out_ref[0] = old_ref[0] + lagged


def lag(arrived, old_rows):
    return pl.pallas_call(
        lag_kernel,
        grid=(PRODUCTS,),
        out_shape=jax.ShapeDtypeStruct((PRODUCTS, PER_OWNER, LAG_BINS), jnp.float32),
        in_specs=[
            pl.BlockSpec((DEVICES, VALUES, PER_OWNER), lambda i: (0, 0, 0)),
            pl.BlockSpec((2 * FREQ_BINS, LAG_BINS), lambda i: (0, 0)),
            pl.BlockSpec((1, PER_OWNER, LAG_BINS), lambda i: (i, 0, 0)),
        ],
        out_specs=pl.BlockSpec((1, PER_OWNER, LAG_BINS), lambda i: (i, 0, 0)),
        compiler_params=pltpu.CompilerParams(vmem_limit_bytes=VMEM_LIMIT),
    )(arrived, jnp.asarray(lag_table()), old_rows)


def local(waveforms, availability, pair_slot, old_stack):
    axes = ("row", "col")
    spectra = whiten(waveforms.reshape(LANES, SAMPLES), availability)
    spectra = lax.all_to_all(spectra, axes, split_axis=0, concat_axis=0, tiled=True)
    crossed = cross(pair_slot.reshape(-1), spectra)
    arrived = lax.all_to_all(crossed, axes, split_axis=0, concat_axis=0, tiled=True)
    old_rows = jnp.transpose(old_stack, (1, 2, 0, 3)).reshape(PRODUCTS, PER_OWNER, LAG_BINS)
    new_rows = lag(arrived, old_rows).reshape(COMPONENTS, COMPONENTS, PER_OWNER, LAG_BINS)
    return jnp.transpose(new_rows, (2, 0, 1, 3))


def solution(mesh):
    return jax.shard_map(
        local,
        mesh=mesh,
        in_specs=(
            P(("row", "col"), None, None, None),
            P(("row", "col"), None),
            P(),
            P(("row", "col"), None, None, None),
        ),
        out_specs=P(("row", "col"), None, None, None),
        check_vma=False,
    )
```

```python
import math

import jax
import jax.numpy as jnp
import ml_dtypes
import numpy as np
from jax import lax
from jax.experimental import pallas as pl
from jax.experimental.pallas import tpu as pltpu
from jax.sharding import PartitionSpec as P

SEGMENTS = 160
COMPONENTS = 3
SAMPLES = 1024
LAG_BINS = 512
BAND_HALF = 64
FREQ_BINS = 512
DEVICES = 128
STATIONS = 128
PER_OWNER = 128
BINS = FREQ_BINS // DEVICES
PARTS = 2 * BINS
LANES = COMPONENTS * SEGMENTS
LANES_FULL = 512
PRODUCTS = COMPONENTS * COMPONENTS
VALUES = PRODUCTS * PARTS
WIDE = -(-8 * VALUES // 128) * 128

EPSILON = 1e-06
VMEM_LIMIT = 56 * 1024 * 1024
NT = (((1,), (1,)), ((), ()))
TN = (((0,), (0,)), ((), ()))


def dft_table():
    turns = np.arange(FREQ_BINS)[:, None] * np.arange(SAMPLES)[None, :] % SAMPLES
    turns = turns.astype(np.float32) * np.float32(2.0 * math.pi / SAMPLES)
    table = np.concatenate([np.cos(turns), -np.sin(turns)], axis=0)
    return table.astype(ml_dtypes.bfloat16)


def band_tables():
    bin_ids = np.arange(FREQ_BINS)
    near = np.abs(bin_ids[:, None] - bin_ids[None, :]) <= BAND_HALF
    return near.astype(ml_dtypes.bfloat16), (1.0 / near.sum(axis=1, keepdims=True)).astype(np.float32)


def lag_table():
    bin_ids = np.arange(FREQ_BINS)
    lag_ids = np.arange(LAG_BINS) - LAG_BINS // 2
    turns = bin_ids[:, None] * lag_ids[None, :] % SAMPLES
    turns = turns.astype(np.float32) * np.float32(2.0 * math.pi / SAMPLES)
    weight = np.where(bin_ids == 0, 1.0, 2.0).astype(np.float32)[:, None] / np.float32(math.sqrt(FREQ_BINS))
    both = np.stack([weight * np.cos(turns), -weight * np.sin(turns)])
    both = both.reshape(2, DEVICES, BINS, LAG_BINS).transpose(1, 0, 2, 3)
    return both.reshape(2 * FREQ_BINS, LAG_BINS).astype(ml_dtypes.bfloat16)


def whiten_kernel(avail_ref, wave_ref, dft_ref, band_ref, share_ref, out_ref, wave_full):
    wave_full[:LANES] = wave_ref[...]
    wave_full[LANES:] = jnp.zeros((LANES_FULL - LANES, SAMPLES), jnp.bfloat16)
    waves = wave_full[...]
    real = lax.dot_general(dft_ref[:FREQ_BINS], waves, NT, preferred_element_type=jnp.float32)
    imag = lax.dot_general(dft_ref[FREQ_BINS:], waves, NT, preferred_element_type=jnp.float32)
    power = real * real + imag * imag
    high = power.astype(jnp.bfloat16)
    low = (power - high.astype(jnp.float32)).astype(jnp.bfloat16)
    band = band_ref[...]
    smooth = jnp.dot(band, high, preferred_element_type=jnp.float32) + jnp.dot(
        band, low, preferred_element_type=jnp.float32
    )
    lane = lax.broadcasted_iota(jnp.int32, (1, LANES_FULL), 1)
    segment = lane % SEGMENTS
    first, last = avail_ref[0, 0], avail_ref[0, 1]
    mask = ((segment >= first) & (segment < last) & (lane < LANES)).astype(jnp.float32)
    factor = lax.rsqrt(smooth * share_ref[...] + EPSILON) * mask
    spare = jnp.where(lane == LANES, first, jnp.where(lane == LANES + 1, last, 0)).astype(jnp.float32)
    real = (real * factor + spare).reshape(FREQ_BINS // 8, 8, LANES_FULL)
    imag = (imag * factor + spare).reshape(FREQ_BINS // 8, 8, LANES_FULL)
    lower = lax.broadcasted_iota(jnp.int32, (1, 8, 1), 1) < BINS
    out_ref[:, 0] = jnp.where(lower, real, pltpu.roll(imag, BINS, 1)).astype(jnp.bfloat16)
    out_ref[:, 1] = jnp.where(lower, pltpu.roll(real, BINS, 1), imag).astype(jnp.bfloat16)


def whiten(waves, availability):
    near, share = band_tables()
    out = pl.pallas_call(
        whiten_kernel,
        out_shape=jax.ShapeDtypeStruct((FREQ_BINS // 8, 2, PARTS, LANES_FULL), jnp.bfloat16),
        in_specs=[pl.BlockSpec(memory_space=pltpu.SMEM)] + [pl.BlockSpec(memory_space=pltpu.VMEM)] * 4,
        out_specs=pl.BlockSpec(memory_space=pltpu.VMEM),
        scratch_shapes=[pltpu.VMEM((LANES_FULL, SAMPLES), jnp.bfloat16)],
        compiler_params=pltpu.CompilerParams(vmem_limit_bytes=VMEM_LIMIT),
    )(availability, waves, jnp.asarray(dft_table()), jnp.asarray(near), jnp.asarray(share))
    return out.reshape(DEVICES, PARTS, LANES_FULL)


def route_kernel(slot_ref, order_ref, place_ref, shift_ref):
    shape = (DEVICES, PER_OWNER)
    tile = lax.broadcasted_iota(jnp.int32, shape, 0)
    lane = lax.broadcasted_iota(jnp.int32, shape, 1)
    slots = slot_ref[...]
    shift = (slots // PER_OWNER - tile) & (DEVICES - 1)
    slot = slots & (PER_OWNER - 1)
    key = shift * PER_OWNER + lane

    def count(i, total):
        for k in range(8):
            total = total + (pltpu.roll(key, i * 8 + k, 1) < key).astype(jnp.int32)
        return total

    rank = lax.fori_loop(0, PER_OWNER // 8, count, jnp.zeros(shape, jnp.int32))
    packed = (rank << 21) | (shift << 14) | (lane << 7) | slot

    def pick(i, found):
        for k in range(8):
            turned = pltpu.roll(packed, i * 8 + k, 1)
            found = jnp.where((turned >> 21) == lane, turned, found)
        return found

    ordered = lax.fori_loop(0, PER_OWNER // 8, pick, jnp.zeros(shape, jnp.int32))
    order_ref[...] = (ordered >> 7) & (PER_OWNER - 1)
    shift = (ordered >> 14) & (DEVICES - 1)
    shift_ref[...] = shift[:8]
    slot = ordered & (PER_OWNER - 1)
    for bit in range(7):
        slot = jnp.where((shift >> bit) & 1 == 1, pltpu.roll(slot, 1 << bit, 0), slot)
    place_ref[...] = slot


def route(pair_slot):
    tiles = pair_slot.reshape(8, 16, 8, 16).transpose(0, 3, 1, 2).reshape(DEVICES, PER_OWNER)
    table = jax.ShapeDtypeStruct((DEVICES, PER_OWNER), jnp.int32)
    return pl.pallas_call(
        route_kernel,
        out_shape=(table, table, jax.ShapeDtypeStruct((8, PER_OWNER), jnp.int32)),
        in_specs=[pl.BlockSpec(memory_space=pltpu.VMEM)],
        out_specs=[pl.BlockSpec(memory_space=pltpu.VMEM)] * 3,
        compiler_params=pltpu.CompilerParams(vmem_limit_bytes=VMEM_LIMIT),
        cost_estimate=pl.CostEstimate(flops=40_000_000, bytes_accessed=200_000, transcendentals=0),
    )(tiles)


def cross_kernel(order_ref, shift_ref, spec_ref, out_ref, spec_full, planes, columns, turned, moved):
    wide = spec_ref[...].astype(jnp.float32).reshape(STATIONS * PARTS, LANES_FULL)
    tiles = LANES_FULL // 128
    for t in range(tiles):
        spec_full[t] = wide[:, t * 128 : (t + 1) * 128]

    def part(row):
        return jnp.concatenate(
            [
                jnp.concatenate(
                    [spec_full[t, pl.ds(low * PARTS + row, 8, stride=16 * PARTS), :] for low in range(16)], axis=0
                )
                for t in range(tiles)
            ],
            axis=1,
        )

    head = part(0)
    first = jnp.broadcast_to(head[:, LANES : LANES + 1], (STATIONS, STATIONS))
    last = jnp.broadcast_to(head[:, LANES + 1 : LANES + 2], (STATIONS, STATIONS))
    counts = jnp.minimum(last, last.T) - jnp.maximum(first, first.T)
    one = lax.broadcasted_iota(jnp.int32, (STATIONS, STATIONS), 0)
    two = lax.broadcasted_iota(jnp.int32, (STATIONS, STATIONS), 1)
    scale = jnp.where(one == two, 0.0, 1.0 / counts)

    def fold(values):
        return jnp.concatenate(
            [values[:, c * SEGMENTS : (c + 1) * SEGMENTS] for c in range(COMPONENTS)], axis=0
        ).astype(jnp.bfloat16)

    def product(x, y):
        return lax.dot_general(x, y, NT, preferred_element_type=jnp.float32)

    for f in range(BINS):
        real, imag = fold(part(f)), fold(part(BINS + f))
        both = (product(real, real) + product(imag, imag), product(imag, real) - product(real, imag))
        for p in range(2):
            for c in range(COMPONENTS):
                for d in range(COMPONENTS):
                    plane = both[p][c * STATIONS : (c + 1) * STATIONS, d * STATIONS : (d + 1) * STATIONS]
                    row = (c * COMPONENTS + d) * PARTS + p * BINS + f
                    planes[pl.ds(row, STATIONS, stride=VALUES), :] = plane * scale

    moves = [(shift_ref[...] >> bit) & 1 == 1 for bit in range(7)]

    def rows_of(tile, cd):
        return pl.ds(pl.multiple_of(tile * VALUES + cd * 8, 8), 8)

    def first_turn(low, carry):
        begin = pl.multiple_of(low * 8 * VALUES, 8)
        for k in range(WIDE // 128):
            count = min(128, 8 * VALUES - k * 128)
            rows = planes[pl.ds(pl.multiple_of(begin + k * 128, 8), count), :]
            columns[low, :, k * 128 : k * 128 + count] = rows.astype(jnp.bfloat16).T.astype(jnp.float32)
        return carry

    lax.fori_loop(0, 16, first_turn, 0, unroll=2)

    pair = lax.broadcasted_iota(jnp.int32, (PER_OWNER, PER_OWNER), 0)

    def second_turn(low, carry):
        for k in range(WIDE // 128):
            count = min(128, 8 * VALUES - k * 128)
            block = columns[:, pl.ds(pl.multiple_of(low * 8, 8), 8), k * 128 : k * 128 + count]
            turned[k * 128 : k * 128 + count, :] = block.reshape(PER_OWNER, count).T
        for high in range(8):
            tile = high * 16 + low
            chosen = jnp.where(pair == order_ref[pl.ds(tile, 1), :], 1.0, 0.0).astype(jnp.bfloat16)
            values = turned[high * VALUES : (high + 1) * VALUES, :].astype(jnp.bfloat16)
            moved[pl.ds(pl.multiple_of(tile * VALUES, 8), VALUES), :] = jnp.dot(
                values, chosen, preferred_element_type=jnp.float32
            )
        return carry

    lax.fori_loop(0, 16, second_turn, 0)

    def shift_eights(residue, carry):
        for cd in range(PRODUCTS):
            x = [moved[rows_of(residue + 8 * i, cd), :] for i in range(16)]
            for bit in range(4):
                x = [jnp.where(moves[3 + bit], x[(i - (1 << bit)) % 16], x[i]) for i in range(16)]
            for i in range(16):
                moved[rows_of(residue + 8 * i, cd), :] = x[i]
        return carry

    lax.fori_loop(0, 8, shift_eights, 0)

    def finish(block, carry):
        for cd in range(PRODUCTS):
            x = [moved[rows_of((block * 16 + DEVICES - 7 + i) & (DEVICES - 1), cd), :] for i in range(23)]
            for bit in range(3):
                step = 1 << bit
                x = [None] * step + [
                    None if x[i - step] is None else jnp.where(moves[bit], x[i - step], x[i]) for i in range(step, 23)
                ]
            for i in range(16):
                planes[rows_of(block * 16 + i, cd), :] = x[7 + i]
        for i in range(16):
            owner = block * 16 + i
            out_ref[owner] = planes[pl.ds(pl.multiple_of(owner * VALUES, 8), VALUES), :].astype(jnp.bfloat16)
        return carry

    lax.fori_loop(0, 8, finish, 0)


def cross(order, shift, spectra):
    return pl.pallas_call(
        cross_kernel,
        out_shape=jax.ShapeDtypeStruct((DEVICES, VALUES, PER_OWNER), jnp.bfloat16),
        in_specs=[pl.BlockSpec(memory_space=pltpu.VMEM)] * 3,
        out_specs=pl.BlockSpec(memory_space=pltpu.VMEM),
        scratch_shapes=[
            pltpu.VMEM((LANES_FULL // 128, STATIONS * PARTS, 128), jnp.float32),
            pltpu.VMEM((STATIONS * VALUES, STATIONS), jnp.float32),
            pltpu.VMEM((16, STATIONS, WIDE), jnp.float32),
            pltpu.VMEM((8 * VALUES, STATIONS), jnp.float32),
            pltpu.VMEM((STATIONS * VALUES, STATIONS), jnp.float32),
        ],
        compiler_params=pltpu.CompilerParams(vmem_limit_bytes=VMEM_LIMIT),
    )(order, shift, spectra)


def lag_kernel(owner_ref, cross_ref, table_ref, place_ref, old_ref, out_ref):
    spectra = cross_ref[...].reshape(2 * FREQ_BINS, PER_OWNER)
    row = lax.broadcasted_iota(jnp.int32, (PER_OWNER, PER_OWNER), 0)
    chosen = jnp.where(row == place_ref[pl.ds(owner_ref[0], 1), :], 1.0, 0.0).astype(jnp.bfloat16)
    rows = lax.dot_general(chosen, spectra, NT, preferred_element_type=jnp.float32).astype(jnp.bfloat16)
    out_ref[0] = old_ref[0] + jnp.dot(rows, table_ref[...], preferred_element_type=jnp.float32)


def lag(owner, arrived, place, old_rows):
    return pl.pallas_call(
        lag_kernel,
        grid=(PRODUCTS,),
        out_shape=jax.ShapeDtypeStruct((PRODUCTS, PER_OWNER, LAG_BINS), jnp.float32),
        in_specs=[
            pl.BlockSpec(memory_space=pltpu.SMEM),
            pl.BlockSpec((DEVICES, PARTS, PER_OWNER), lambda i: (0, i, 0)),
            pl.BlockSpec((2 * FREQ_BINS, LAG_BINS), lambda i: (0, 0)),
            pl.BlockSpec((DEVICES, PER_OWNER), lambda i: (0, 0)),
            pl.BlockSpec((1, PER_OWNER, LAG_BINS), lambda i: (i, 0, 0)),
        ],
        out_specs=pl.BlockSpec((1, PER_OWNER, LAG_BINS), lambda i: (i, 0, 0)),
        compiler_params=pltpu.CompilerParams(vmem_limit_bytes=VMEM_LIMIT),
    )(owner, arrived, jnp.asarray(lag_table()), place, old_rows)


def local(waveforms, availability, pair_slot, old_stack):
    axes = ("row", "col")
    spectra = whiten(waveforms.reshape(LANES, SAMPLES), availability)
    spectra = lax.all_to_all(spectra, axes, split_axis=0, concat_axis=0, tiled=True)
    order, place, shift = route(pair_slot)
    crossed = cross(order, shift, spectra)
    arrived = lax.all_to_all(crossed, axes, split_axis=0, concat_axis=0, tiled=True)
    old_rows = jnp.transpose(old_stack, (1, 2, 0, 3)).reshape(PRODUCTS, PER_OWNER, LAG_BINS)
    owner = (lax.axis_index("row") * lax.axis_size("col") + lax.axis_index("col")).astype(jnp.int32).reshape(1)
    new_rows = lag(owner, arrived, place, old_rows).reshape(COMPONENTS, COMPONENTS, PER_OWNER, LAG_BINS)
    return jnp.transpose(new_rows, (2, 0, 1, 3))


def solution(mesh):
    return jax.shard_map(
        local,
        mesh=mesh,
        in_specs=(
            P(("row", "col"), None, None, None),
            P(("row", "col"), None),
            P(),
            P(("row", "col"), None, None, None),
        ),
        out_specs=P(("row", "col"), None, None, None),
        check_vma=False,
    )
```

```python
import math

import jax
import jax.numpy as jnp
import ml_dtypes
import numpy as np
from jax import lax
from jax.experimental import pallas as pl
from jax.experimental.pallas import tpu as pltpu
from jax.sharding import PartitionSpec as P

SEGMENTS = 160
COMPONENTS = 3
SAMPLES = 1024
LAG_BINS = 512
BAND_HALF = 64
FREQ_BINS = 512
DEVICES = 128
STATIONS = 128
PER_OWNER = 128
BINS = FREQ_BINS // DEVICES
PARTS = 2 * BINS
LANES = COMPONENTS * SEGMENTS
LANES_FULL = 512
PRODUCTS = COMPONENTS * COMPONENTS
VALUES = PRODUCTS * PARTS
ROWS = -(-VALUES // 16) * 16
APART = ROWS + 8
WIDE = 8 * ROWS

LEAVE = 32

EPSILON = 1e-06
MIB = 1024 * 1024
NT = (((1,), (1,)), ((), ()))
TN = (((0,), (0,)), ((), ()))


def dft_table():
    turns = np.arange(FREQ_BINS)[:, None] * np.arange(SAMPLES)[None, :] % SAMPLES
    turns = turns.astype(np.float32) * np.float32(2.0 * math.pi / SAMPLES)
    table = np.concatenate([np.cos(turns), -np.sin(turns)], axis=0)
    return table.astype(ml_dtypes.bfloat16)


def band_table():
    bin_ids = np.arange(FREQ_BINS)
    return (np.abs(bin_ids[:, None] - bin_ids[None, :]) <= BAND_HALF).astype(ml_dtypes.bfloat16)


def lag_table():
    bin_ids = np.arange(FREQ_BINS)
    lag_ids = np.arange(LAG_BINS) - LAG_BINS // 2
    turns = bin_ids[:, None] * lag_ids[None, :] % SAMPLES
    turns = turns.astype(np.float32) * np.float32(2.0 * math.pi / SAMPLES)
    weight = np.where(bin_ids == 0, 1.0, 2.0).astype(np.float32)[:, None] / np.float32(math.sqrt(FREQ_BINS))
    both = np.stack([weight * np.cos(turns), -weight * np.sin(turns)])
    return both.transpose(1, 0, 2).reshape(2 * FREQ_BINS, LAG_BINS).astype(ml_dtypes.bfloat16)


def lane_runs():
    whole = [(c * SEGMENTS, c * 128, 128) for c in range(COMPONENTS)]
    rest = SEGMENTS - 128
    return whole + [(c * SEGMENTS + 128, COMPONENTS * 128 + c * rest, rest) for c in range(COMPONENTS)]


def whiten_kernel(
    avail_hbm, wave_hbm, dft_hbm, band_hbm, out_ref, avail, wave, dft, band, mixed, avail_sem, wave_sems, dft_sems, band_sem
):
    runs = lane_runs()
    wave_copies = [
        pltpu.make_async_copy(wave_hbm.at[pl.ds(row, count)], wave.at[pl.ds(begin, count)], wave_sems.at[i])
        for i, (row, begin, count) in enumerate(runs)
    ]
    dft_copies = [
        pltpu.make_async_copy(
            dft_hbm.at[pl.ds(i * FREQ_BINS, FREQ_BINS)], dft.at[pl.ds(i * FREQ_BINS, FREQ_BINS)], dft_sems.at[i]
        )
        for i in range(2)
    ]
    band_copy = pltpu.make_async_copy(band_hbm, band, band_sem)
    avail_copy = pltpu.make_async_copy(avail_hbm, avail, avail_sem)
    for copy in wave_copies + dft_copies + [band_copy, avail_copy]:
        copy.start()
    wave[LANES:] = jnp.zeros((LANES_FULL - LANES, SAMPLES), jnp.bfloat16)
    for copy in wave_copies:
        copy.wait()
    waves = wave[...].T
    dft_copies[0].wait()
    real = jnp.dot(dft[:FREQ_BINS], waves, preferred_element_type=jnp.float32)
    dft_copies[1].wait()
    imag = jnp.dot(dft[FREQ_BINS:], waves, preferred_element_type=jnp.float32)
    power = real * real + imag * imag
    high = power.astype(jnp.bfloat16)
    low = (power - high.astype(jnp.float32)).astype(jnp.bfloat16)
    band_copy.wait()
    near = band[...]
    smooth = jnp.dot(near, high, preferred_element_type=jnp.float32) + jnp.dot(
        near, low, preferred_element_type=jnp.float32
    )
    bin_id = lax.broadcasted_iota(jnp.int32, (FREQ_BINS, 1), 0)
    width = jnp.minimum(bin_id, BAND_HALF) + jnp.minimum(FREQ_BINS - 1 - bin_id, BAND_HALF) + 1
    lane = lax.broadcasted_iota(jnp.int32, (1, LANES_FULL), 1)
    segment = jnp.where(lane < COMPONENTS * 128, lane & 127, 128 + (lane & (SEGMENTS - 129)))
    avail_copy.wait()
    first, last = avail[0, 0], avail[0, 1]
    mask = ((segment >= first) & (segment < last) & (lane < LANES)).astype(jnp.float32)
    factor = lax.rsqrt(smooth * (1.0 / width.astype(jnp.float32)) + EPSILON) * mask
    spare = jnp.where(lane == LANES, first, jnp.where(lane == LANES + 1, last, 0)).astype(jnp.float32)
    real = real * factor + spare
    imag = imag * factor + spare
    for t in range(LANES_FULL // 128):
        mixed[t, pl.ds(0, FREQ_BINS, stride=2), :] = real[:, t * 128 : (t + 1) * 128]
        mixed[t, pl.ds(1, FREQ_BINS, stride=2), :] = imag[:, t * 128 : (t + 1) * 128]
    for t in range(LANES_FULL // 128):
        out_ref[:, :, t * 128 : (t + 1) * 128] = mixed[t].astype(jnp.bfloat16).reshape(DEVICES, PARTS, 128)


def whiten(waves, availability):
    in_hbm = (availability, waves, jnp.asarray(dft_table()), jnp.asarray(band_table()))
    return pl.pallas_call(
        whiten_kernel,
        out_shape=jax.ShapeDtypeStruct((DEVICES, PARTS, LANES_FULL), jnp.bfloat16),
        in_specs=[pl.BlockSpec(memory_space=pltpu.HBM)] * 4,
        out_specs=pl.BlockSpec(memory_space=pltpu.VMEM),
        scratch_shapes=[
            pltpu.SMEM((1, 2), jnp.int32),
            pltpu.VMEM((LANES_FULL, SAMPLES), jnp.bfloat16),
            pltpu.VMEM((2 * FREQ_BINS, SAMPLES), jnp.bfloat16),
            pltpu.VMEM((FREQ_BINS, FREQ_BINS), jnp.bfloat16),
            pltpu.VMEM((LANES_FULL // 128, 2 * FREQ_BINS, 128), jnp.float32),
            pltpu.SemaphoreType.DMA,
            pltpu.SemaphoreType.DMA((2 * COMPONENTS,)),
            pltpu.SemaphoreType.DMA((2,)),
            pltpu.SemaphoreType.DMA,
        ],
        compiler_params=pltpu.CompilerParams(vmem_limit_bytes=20 * MIB),
    )(*(pltpu.with_memory_space_constraint(x, pltpu.HBM) for x in in_hbm))


def route_kernel(slot_ref, order_ref, place_ref, shift_ref):
    shape = (DEVICES, PER_OWNER)
    tile = lax.broadcasted_iota(jnp.int32, shape, 0)
    lane = lax.broadcasted_iota(jnp.int32, shape, 1)
    slots = slot_ref[...]
    shift = (slots // PER_OWNER - tile) & (DEVICES - 1)
    slot = slots & (PER_OWNER - 1)
    key = shift * PER_OWNER + lane

    def count(i, total):
        for k in range(8):
            total = total + (pltpu.roll(key, i * 8 + k, 1) < key).astype(jnp.int32)
        return total

    rank = lax.fori_loop(0, PER_OWNER // 8, count, jnp.zeros(shape, jnp.int32))
    packed = (rank << 21) | (shift << 14) | (lane << 7) | slot

    def pick(i, found):
        for k in range(8):
            turned = pltpu.roll(packed, i * 8 + k, 1)
            found = jnp.where((turned >> 21) == lane, turned, found)
        return found

    ordered = lax.fori_loop(0, PER_OWNER // 8, pick, jnp.zeros(shape, jnp.int32))
    order_ref[...] = (ordered >> 7) & (PER_OWNER - 1)
    shift = (ordered >> 14) & (DEVICES - 1)
    shift_ref[...] = shift[:8]
    slot = ordered & (PER_OWNER - 1)
    for bit in range(7):
        slot = jnp.where((shift >> bit) & 1 == 1, pltpu.roll(slot, 1 << bit, 0), slot)
    place_ref[...] = slot


def route(pair_slot):
    tiles = pair_slot.reshape(8, 16, 8, 16).transpose(0, 3, 1, 2).reshape(DEVICES, PER_OWNER)
    table = jax.ShapeDtypeStruct((DEVICES, PER_OWNER), jnp.int32)
    return pl.pallas_call(
        route_kernel,
        out_shape=(table, table, jax.ShapeDtypeStruct((8, PER_OWNER), jnp.int32)),
        in_specs=[pl.BlockSpec(memory_space=pltpu.VMEM)],
        out_specs=[pl.BlockSpec(memory_space=pltpu.VMEM)] * 3,
        compiler_params=pltpu.CompilerParams(vmem_limit_bytes=4 * MIB),
        cost_estimate=pl.CostEstimate(flops=40_000_000, bytes_accessed=200_000, transcendentals=0),
    )(tiles)


def cross_kernel(
    order_ref, shift_ref, spec_ref, out_hbm, spec_full, planes, columns, turned, placed, moved, ready, out_sems
):
    wide = spec_ref[...].astype(jnp.float32).reshape(STATIONS * PARTS, LANES_FULL)
    tiles = LANES_FULL // 128
    for t in range(tiles):
        spec_full[t] = wide[:, t * 128 : (t + 1) * 128]

    def part(row, t):
        return jnp.concatenate(
            [spec_full[t, pl.ds(low * PARTS + row, 8, stride=16 * PARTS), :] for low in range(16)], axis=0
        )

    head = part(0, LANES // 128)
    spare = LANES % 128
    first = jnp.broadcast_to(head[:, spare : spare + 1], (STATIONS, STATIONS))
    last = jnp.broadcast_to(head[:, spare + 1 : spare + 2], (STATIONS, STATIONS))
    counts = jnp.minimum(last, last.T) - jnp.maximum(first, first.T)
    one = lax.broadcasted_iota(jnp.int32, (STATIONS, STATIONS), 0)
    two = lax.broadcasted_iota(jnp.int32, (STATIONS, STATIONS), 1)
    scale = jnp.where(one == two, 0.0, 1.0 / counts)

    def fold(row):
        pieces = [part(row, t).astype(jnp.bfloat16) for t in range(tiles)]
        rest = SEGMENTS - 128
        return jnp.concatenate(
            [
                jnp.concatenate([pieces[c], pieces[-1][:, c * rest : (c + 1) * rest]], axis=1)
                for c in range(COMPONENTS)
            ],
            axis=0,
        )

    def product(x, y):
        return jnp.dot(x, y, preferred_element_type=jnp.float32)

    for f in range(BINS):
        real, imag = fold(2 * f), fold(2 * f + 1)
        real_t, imag_t = real.T, imag.T
        both = (product(real, real_t) + product(imag, imag_t), product(imag, real_t) - product(real, imag_t))
        for p in range(2):
            for c in range(COMPONENTS):
                for d in range(COMPONENTS):
                    plane = both[p][c * STATIONS : (c + 1) * STATIONS, d * STATIONS : (d + 1) * STATIONS]
                    row = (c * COMPONENTS + d) * PARTS + 2 * f + p
                    planes[pl.ds(row, STATIONS, stride=APART), :] = plane * scale

    moves = [(shift_ref[...] >> bit) & 1 == 1 for bit in range(7)]

    def first_turn(i, carry):
        two = 16 * APART
        source = planes.at[pl.ds(pl.multiple_of(i * two, 8), two)]
        target = columns.at[:, pl.ds(pl.multiple_of(i * 16, 16), 16)]
        for k in range(WIDE // 128):
            sides = []
            for side in range(2):
                rows = []
                for begin in range(k * 128, (k + 1) * 128, 8):
                    high, value = divmod(begin, ROWS)
                    row = (side * 8 + high) * APART + value
                    rows.append(source[row : row + 8, :])
                rows = jnp.concatenate(rows, axis=0).astype(jnp.bfloat16).T
                sides.append(rows.astype(jnp.float32).reshape(16, 8, 128))
            target[:, :, k * 128 : (k + 1) * 128] = jnp.concatenate(sides, axis=1).astype(jnp.bfloat16)
        return carry

    lax.fori_loop(0, 8, first_turn, 0, unroll=2)

    pair = lax.broadcasted_iota(jnp.int32, (PER_OWNER, PER_OWNER), 0)

    def second_turn(i, carry):
        source = columns.at[pl.ds(2 * i, 2)]
        for side in range(2):
            for k in range(WIDE // 128):
                turned[side, k * 128 : (k + 1) * 128, :] = source[side, :, k * 128 : (k + 1) * 128].T
        targets = [moved.at[pl.ds(high * 16 + 2 * i, 2)] for high in range(9)]
        for side in range(2):
            for high in range(8):
                order = order_ref[pl.ds(high * 16 + 2 * i + side, 1), :]
                chosen = jnp.where(pair == order, 1.0, 0.0).astype(jnp.bfloat16)
                values = turned[side, high * ROWS : (high + 1) * ROWS, :]
                placed[side, high * ROWS : (high + 1) * ROWS, :] = jnp.dot(
                    values, chosen, preferred_element_type=jnp.float32
                )
            for group in range(0, VALUES, 8):
                x = [placed[side, high * ROWS + group : high * ROWS + group + 8, :] for high in range(8)]
                for bit in range(3):
                    x = [jnp.where(moves[4 + bit], x[(high - (1 << bit)) % 8], x[high]) for high in range(8)]
                for high in range(9):
                    targets[high][side, group : group + 8, :] = x[(high - 1) % 8]
        return carry

    lax.fori_loop(0, 8, second_turn, 0)

    def leave(block):
        some = pl.ds(pl.multiple_of(block * LEAVE, LEAVE), LEAVE)
        return pltpu.make_async_copy(ready.at[some], out_hbm.at[some], out_sems.at[block])

    def finish(block, carry):
        source = moved.at[pl.ds(block * LEAVE + 1, LEAVE + 15)]
        target = ready.at[pl.ds(block * LEAVE, LEAVE)]
        for group in range(0, VALUES, 8):
            x = [source[i, group : group + 8, :] for i in range(LEAVE + 15)]
            for bit in reversed(range(4)):
                step = 1 << bit
                x = [jnp.where(moves[bit], x[i - step], x[i]) for i in range(step, len(x))]
            for i in range(LEAVE):
                target[i, group : group + 8, :] = x[i].astype(jnp.bfloat16)
        leave(block).start()
        return carry

    lax.fori_loop(0, DEVICES // LEAVE, finish, 0)
    for block in range(DEVICES // LEAVE):
        leave(block).wait()


def cross(order, shift, spectra):
    return pl.pallas_call(
        cross_kernel,
        out_shape=jax.ShapeDtypeStruct((DEVICES, VALUES, PER_OWNER), jnp.bfloat16),
        in_specs=[pl.BlockSpec(memory_space=pltpu.VMEM)] * 3,
        out_specs=pl.BlockSpec(memory_space=pltpu.HBM),
        scratch_shapes=[
            pltpu.VMEM((LANES_FULL // 128, STATIONS * PARTS, 128), jnp.float32),
            pltpu.VMEM((STATIONS * APART, STATIONS), jnp.float32),
            pltpu.VMEM((16, STATIONS, WIDE), jnp.bfloat16),
            pltpu.VMEM((2, WIDE, STATIONS), jnp.bfloat16),
            pltpu.VMEM((2, WIDE, STATIONS), jnp.float32),
            pltpu.VMEM((DEVICES + 16, VALUES, PER_OWNER), jnp.float32),
            pltpu.VMEM((DEVICES, VALUES, PER_OWNER), jnp.bfloat16),
            pltpu.SemaphoreType.DMA((DEVICES // LEAVE,)),
        ],
        compiler_params=pltpu.CompilerParams(vmem_limit_bytes=28 * MIB),
    )(order, shift, spectra)


def lag_kernel(owner_ref, cross_ref, table_ref, place_ref, old_hbm, out_hbm, old, new, old_sems, new_sems):
    old_copies = [pltpu.make_async_copy(old_hbm.at[c], old.at[c], old_sems.at[c]) for c in range(COMPONENTS)]
    new_copies = [pltpu.make_async_copy(new.at[c], out_hbm.at[c], new_sems.at[c]) for c in range(COMPONENTS)]
    for copy in old_copies:
        copy.start()
    row = lax.broadcasted_iota(jnp.int32, (PER_OWNER, PER_OWNER), 0)
    chosen = jnp.where(row == place_ref[pl.ds(owner_ref[0], 1), :], 1.0, 0.0).astype(jnp.bfloat16)
    for c in range(COMPONENTS):
        rows = []
        for cd in range(c * COMPONENTS, (c + 1) * COMPONENTS):
            spectra = cross_ref[:, cd * PARTS : (cd + 1) * PARTS, :].reshape(2 * FREQ_BINS, PER_OWNER)
            turned = lax.dot_general(chosen, spectra, NT, preferred_element_type=jnp.float32)
            rows.append(turned.astype(jnp.bfloat16))
        lagged = jnp.dot(jnp.concatenate(rows, axis=0), table_ref[...], preferred_element_type=jnp.float32)
        old_copies[c].wait()
        new[c] = old[c] + lagged.reshape(COMPONENTS, PER_OWNER, LAG_BINS)
        new_copies[c].start()
    for copy in new_copies:
        copy.wait()


def lag(owner, arrived, place, old_rows):
    shape = (COMPONENTS, COMPONENTS, PER_OWNER, LAG_BINS)
    return pl.pallas_call(
        lag_kernel,
        out_shape=jax.ShapeDtypeStruct(shape, jnp.float32),
        in_specs=[pl.BlockSpec(memory_space=pltpu.SMEM)]
        + [pl.BlockSpec(memory_space=pltpu.VMEM)] * 3
        + [pl.BlockSpec(memory_space=pltpu.HBM)],
        out_specs=pl.BlockSpec(memory_space=pltpu.HBM),
        scratch_shapes=[
            pltpu.VMEM(shape, jnp.float32),
            pltpu.VMEM(shape, jnp.float32),
            pltpu.SemaphoreType.DMA((COMPONENTS,)),
            pltpu.SemaphoreType.DMA((COMPONENTS,)),
        ],
        compiler_params=pltpu.CompilerParams(vmem_limit_bytes=24 * MIB),
    )(owner, arrived, jnp.asarray(lag_table()), place, pltpu.with_memory_space_constraint(old_rows, pltpu.HBM))


def local(waveforms, availability, pair_slot, old_stack):
    axes = ("row", "col")
    spectra = whiten(waveforms.reshape(LANES, SAMPLES), availability)
    spectra = lax.all_to_all(spectra, axes, split_axis=0, concat_axis=0, tiled=True)
    order, place, shift = route(pair_slot)
    crossed = cross(order, shift, spectra)
    arrived = lax.all_to_all(crossed, axes, split_axis=0, concat_axis=0, tiled=True)
    old_rows = jnp.transpose(old_stack, (1, 2, 0, 3))
    owner = (lax.axis_index("row") * lax.axis_size("col") + lax.axis_index("col")).astype(jnp.int32).reshape(1)
    return jnp.transpose(lag(owner, arrived, place, old_rows), (2, 0, 1, 3))


def solution(mesh):
    return jax.shard_map(
        local,
        mesh=mesh,
        in_specs=(
            P(("row", "col"), None, None, None),
            P(("row", "col"), None),
            P(),
            P(("row", "col"), None, None, None),
        ),
        out_specs=P(("row", "col"), None, None, None),
        check_vma=False,
    )
```

```python
import math

import jax
import jax.numpy as jnp
import ml_dtypes
import numpy as np
from jax import lax
from jax.experimental import pallas as pl
from jax.experimental.pallas import tpu as pltpu
from jax.sharding import PartitionSpec as P

SEGMENTS = 160
COMPONENTS = 3
SAMPLES = 1024
LAG_BINS = 512
BAND_HALF = 64
FREQ_BINS = 512
DEVICES = 128
STATIONS = 128
PER_OWNER = 128
BINS = FREQ_BINS // DEVICES
PARTS = 2 * BINS
LANES = COMPONENTS * SEGMENTS
LANES_FULL = 512
PRODUCTS = COMPONENTS * COMPONENTS
VALUES = PRODUCTS * PARTS
ROWS = -(-VALUES // 16) * 16
APART = ROWS + 8
SIXTEEN = 16 * PARTS + 8
WIDE = 8 * ROWS

WHITEN_PIECES = 4
LEAVE = 32

EPSILON = 1e-06
MIB = 1024 * 1024
NT = (((1,), (1,)), ((), ()))
TN = (((0,), (0,)), ((), ()))


def bin_order():
    half = FREQ_BINS // 2
    return np.concatenate([np.arange(half + 1), np.arange(FREQ_BINS - 1, half, -1)])


def dft_table():
    half = FREQ_BINS // 2
    turns = np.arange(half + 1)[:, None] * np.arange(SAMPLES)[None, :] % SAMPLES
    turns = turns.astype(np.float32) * np.float32(2.0 * math.pi / SAMPLES)
    cosine, sine = np.cos(turns), -np.sin(turns)
    fill = np.zeros((14, SAMPLES), np.float32)
    table = np.concatenate([cosine[:half], sine[:half], cosine[half:], sine[half:], fill], axis=0)
    return table.astype(ml_dtypes.bfloat16)


def lag_table():
    bin_ids = bin_order()
    lag_ids = np.arange(LAG_BINS) - LAG_BINS // 2
    turns = bin_ids[:, None] * lag_ids[None, :] % SAMPLES
    turns = turns.astype(np.float32) * np.float32(2.0 * math.pi / SAMPLES)
    weight = np.where(bin_ids == 0, 1.0, 2.0).astype(np.float32)[:, None] / np.float32(math.sqrt(FREQ_BINS))
    both = np.stack([weight * np.cos(turns), -weight * np.sin(turns)])
    return both.transpose(1, 0, 2).reshape(2 * FREQ_BINS, LAG_BINS).astype(ml_dtypes.bfloat16)


def lane_runs():
    whole = [(c * SEGMENTS, c * 128, 128) for c in range(COMPONENTS)]
    rest = SEGMENTS - 128
    return whole + [(c * SEGMENTS + 128, COMPONENTS * 128 + c * rest, rest) for c in range(COMPONENTS)]


def whiten_kernel(
    avail_hbm, wave_hbm, dft_hbm, out_hbm, avail, wave, half_dft, dft, mixed, ready, avail_sem, wave_sems, dft_sems, out_sems
):
    half = FREQ_BINS // 2
    wave_copies = [
        pltpu.make_async_copy(wave_hbm.at[pl.ds(row, count)], wave.at[pl.ds(begin, count)], wave_sems.at[i])
        for i, (row, begin, count) in enumerate(lane_runs())
    ]
    dft_runs = [(p * half, half) for p in range(2)] + [(2 * half, 16)]
    dft_copies = [
        pltpu.make_async_copy(dft_hbm.at[pl.ds(row, count)], half_dft.at[pl.ds(row, count)], dft_sems.at[i])
        for i, (row, count) in enumerate(dft_runs)
    ]
    avail_copy = pltpu.make_async_copy(avail_hbm, avail, avail_sem)
    for copy in wave_copies + dft_copies + [avail_copy]:
        copy.start()
    wave[LANES:] = jnp.zeros((LANES_FULL - LANES, SAMPLES), jnp.bfloat16)

    def bin_of(row):
        return jnp.where(row <= half, row, 3 * half - row)

    square = (FREQ_BINS, FREQ_BINS)
    apart = bin_of(lax.broadcasted_iota(jnp.int32, square, 0)) - bin_of(lax.broadcasted_iota(jnp.int32, square, 1))
    near = jnp.where(jnp.abs(apart) <= BAND_HALF, 1.0, 0.0).astype(jnp.bfloat16)
    for copy in wave_copies:
        copy.wait()
    waves = wave[...].T
    odd = lax.broadcasted_iota(jnp.int32, (half, SAMPLES), 1) & 1 == 1
    top = lax.broadcasted_iota(jnp.int32, (half, SAMPLES), 0) == 0
    for copy in dft_copies:
        copy.wait()
    for p in range(2):
        lower = half_dft[p * half : (p + 1) * half]
        middle = half_dft[2 * half : 2 * half + 16][p : p + 1]
        mirrored = jnp.where(odd, -lower, lower) if p == 0 else jnp.where(odd, lower, -lower)
        dft[p * FREQ_BINS : p * FREQ_BINS + half] = lower
        dft[p * FREQ_BINS + half : (p + 1) * FREQ_BINS] = jnp.where(top, middle, mirrored)
    real = jnp.dot(dft[:FREQ_BINS], waves, preferred_element_type=jnp.float32)
    imag = jnp.dot(dft[FREQ_BINS:], waves, preferred_element_type=jnp.float32)
    power = real * real + imag * imag
    high = power.astype(jnp.bfloat16)
    low = (power - high.astype(jnp.float32)).astype(jnp.bfloat16)
    smooth = jnp.dot(near, high, preferred_element_type=jnp.float32) + jnp.dot(
        near, low, preferred_element_type=jnp.float32
    )
    bin_id = bin_of(lax.broadcasted_iota(jnp.int32, (FREQ_BINS, 1), 0))
    width = jnp.minimum(bin_id, BAND_HALF) + jnp.minimum(FREQ_BINS - 1 - bin_id, BAND_HALF) + 1
    lane = lax.broadcasted_iota(jnp.int32, (1, LANES_FULL), 1)
    segment = jnp.where(lane < COMPONENTS * 128, lane & 127, 128 + (lane & (SEGMENTS - 129)))
    avail_copy.wait()
    first, last = avail[0, 0], avail[0, 1]
    mask = ((segment >= first) & (segment < last) & (lane < LANES)).astype(jnp.float32)
    factor = lax.rsqrt(smooth * (1.0 / width.astype(jnp.float32)) + EPSILON) * mask
    spare = jnp.where(lane == LANES, first, jnp.where(lane == LANES + 1, last, 0)).astype(jnp.float32)
    out_copies = []
    bins = FREQ_BINS // WHITEN_PIECES
    for i in range(WHITEN_PIECES):
        rows = slice(i * bins, (i + 1) * bins)
        for p, values in enumerate((real[rows] * factor[rows] + spare, imag[rows] * factor[rows] + spare)):
            for t in range(LANES_FULL // 128):
                mixed[t, pl.ds(2 * i * bins + p, bins, stride=2), :] = values[:, t * 128 : (t + 1) * 128]
        some = pl.ds(i * bins // BINS, bins // BINS)
        for t in range(LANES_FULL // 128):
            values = mixed[t, 2 * i * bins : 2 * (i + 1) * bins, :].astype(jnp.bfloat16)
            ready[some, :, t * 128 : (t + 1) * 128] = values.reshape(bins // BINS, PARTS, 128)
        out_copies.append(pltpu.make_async_copy(ready.at[some], out_hbm.at[some], out_sems.at[i]))
        out_copies[i].start()
    for copy in out_copies:
        copy.wait()


def whiten(waves, availability):
    return pl.pallas_call(
        whiten_kernel,
        out_shape=jax.ShapeDtypeStruct((DEVICES, PARTS, LANES_FULL), jnp.bfloat16),
        in_specs=[pl.BlockSpec(memory_space=pltpu.HBM)] * 3,
        out_specs=pl.BlockSpec(memory_space=pltpu.HBM),
        scratch_shapes=[
            pltpu.SMEM((1, 2), jnp.int32),
            pltpu.VMEM((LANES_FULL, SAMPLES), jnp.bfloat16),
            pltpu.VMEM((FREQ_BINS + 16, SAMPLES), jnp.bfloat16),
            pltpu.VMEM((2 * FREQ_BINS, SAMPLES), jnp.bfloat16),
            pltpu.VMEM((LANES_FULL // 128, 2 * FREQ_BINS, 128), jnp.float32),
            pltpu.VMEM((DEVICES, PARTS, LANES_FULL), jnp.bfloat16),
            pltpu.SemaphoreType.DMA,
            pltpu.SemaphoreType.DMA((2 * COMPONENTS,)),
            pltpu.SemaphoreType.DMA((3,)),
            pltpu.SemaphoreType.DMA((WHITEN_PIECES,)),
        ],
        compiler_params=pltpu.CompilerParams(vmem_limit_bytes=24 * MIB),
    )(*(pltpu.with_memory_space_constraint(x, pltpu.HBM) for x in (availability, waves, jnp.asarray(dft_table()))))


def route_kernel(slot_ref, order_ref, place_ref, shift_ref):
    shape = (DEVICES, PER_OWNER)
    tile = lax.broadcasted_iota(jnp.int32, shape, 0)
    lane = lax.broadcasted_iota(jnp.int32, shape, 1)
    slots = slot_ref[...]
    shift = (slots // PER_OWNER - tile) & (DEVICES - 1)
    slot = slots & (PER_OWNER - 1)
    key = shift * PER_OWNER + lane

    def count(i, total):
        for k in range(8):
            total = total + (pltpu.roll(key, i * 8 + k, 1) < key).astype(jnp.int32)
        return total

    rank = lax.fori_loop(0, PER_OWNER // 8, count, jnp.zeros(shape, jnp.int32))
    packed = (rank << 21) | (shift << 14) | (lane << 7) | slot

    def pick(i, found):
        for k in range(8):
            turned = pltpu.roll(packed, i * 8 + k, 1)
            found = jnp.where((turned >> 21) == lane, turned, found)
        return found

    ordered = lax.fori_loop(0, PER_OWNER // 8, pick, jnp.zeros(shape, jnp.int32))
    order_ref[...] = (ordered >> 7) & (PER_OWNER - 1)
    shift = (ordered >> 14) & (DEVICES - 1)
    shift_ref[...] = shift[:8]
    slot = ordered & (PER_OWNER - 1)
    for bit in range(7):
        slot = jnp.where((shift >> bit) & 1 == 1, pltpu.roll(slot, 1 << bit, 0), slot)
    place_ref[...] = slot


def route(pair_slot):
    tiles = pair_slot.reshape(8, 16, 8, 16).transpose(0, 3, 1, 2).reshape(DEVICES, PER_OWNER)
    table = jax.ShapeDtypeStruct((DEVICES, PER_OWNER), jnp.int32)
    return pl.pallas_call(
        route_kernel,
        out_shape=(table, table, jax.ShapeDtypeStruct((8, PER_OWNER), jnp.int32)),
        in_specs=[pl.BlockSpec(memory_space=pltpu.VMEM)],
        out_specs=[pl.BlockSpec(memory_space=pltpu.VMEM)] * 3,
        compiler_params=pltpu.CompilerParams(vmem_limit_bytes=4 * MIB),
        cost_estimate=pl.CostEstimate(flops=40_000_000, bytes_accessed=200_000, transcendentals=0),
    )(tiles)


def cross_kernel(
    order_ref, shift_ref, spec_ref, out_hbm, spec_full, planes, columns, turned, placed, moved, ready, out_sems
):
    wide = spec_ref[...].astype(jnp.float32).reshape(STATIONS * PARTS, LANES_FULL)
    tiles = LANES_FULL // 128
    for t in range(tiles):
        for high in range(8):
            rows = wide[high * 16 * PARTS : (high + 1) * 16 * PARTS, t * 128 : (t + 1) * 128]
            spec_full[t, high * SIXTEEN : high * SIXTEEN + 16 * PARTS] = rows

    def part(row, t):
        return jnp.concatenate(
            [spec_full[t, pl.ds(low * PARTS + row, 8, stride=SIXTEEN), :] for low in range(16)], axis=0
        )

    head = part(0, LANES // 128)
    spare = LANES % 128
    first = jnp.broadcast_to(head[:, spare : spare + 1], (STATIONS, STATIONS))
    last = jnp.broadcast_to(head[:, spare + 1 : spare + 2], (STATIONS, STATIONS))
    counts = jnp.minimum(last, last.T) - jnp.maximum(first, first.T)
    one = lax.broadcasted_iota(jnp.int32, (STATIONS, STATIONS), 0)
    two = lax.broadcasted_iota(jnp.int32, (STATIONS, STATIONS), 1)
    scale = jnp.where(one == two, 0.0, 1.0 / counts)

    def fold(row):
        pieces = [part(row, t).astype(jnp.bfloat16) for t in range(tiles)]
        rest = SEGMENTS - 128
        return jnp.concatenate(
            [
                jnp.concatenate([pieces[c], pieces[-1][:, c * rest : (c + 1) * rest]], axis=1)
                for c in range(COMPONENTS)
            ],
            axis=0,
        )

    def product(x, y):
        return jnp.dot(x, y, preferred_element_type=jnp.float32)

    for f in range(BINS):
        real, imag = fold(2 * f), fold(2 * f + 1)
        real_t, imag_t = real.T, imag.T
        stacked = jnp.concatenate([real, imag], axis=0)
        by_real, by_imag = product(stacked, real_t), product(stacked, imag_t)
        size = COMPONENTS * STATIONS
        both = (by_real[:size] + by_imag[size:], by_real[size:] - by_imag[:size])
        for p in range(2):
            for c in range(COMPONENTS):
                for d in range(COMPONENTS):
                    plane = both[p][c * STATIONS : (c + 1) * STATIONS, d * STATIONS : (d + 1) * STATIONS]
                    row = (c * COMPONENTS + d) * PARTS + 2 * f + p
                    planes[pl.ds(row, STATIONS, stride=APART), :] = plane * scale

    moves = [(shift_ref[...] >> bit) & 1 == 1 for bit in range(7)]

    def first_turn(i, carry):
        two = 16 * APART
        source = planes.at[pl.ds(pl.multiple_of(i * two, 8), two)]
        target = columns.at[:, pl.ds(pl.multiple_of(i * 16, 16), 16)]
        for k in range(WIDE // 128):
            sides = []
            for side in range(2):
                rows = []
                for begin in range(k * 128, (k + 1) * 128, 8):
                    high, value = divmod(begin, ROWS)
                    row = (side * 8 + high) * APART + value
                    rows.append(source[row : row + 8, :])
                rows = jnp.concatenate(rows, axis=0).astype(jnp.bfloat16).T
                sides.append(rows.astype(jnp.float32).reshape(16, 8, 128))
            target[:, :, k * 128 : (k + 1) * 128] = jnp.concatenate(sides, axis=1).astype(jnp.bfloat16)
        return carry

    lax.fori_loop(0, 8, first_turn, 0, unroll=8)

    pair = lax.broadcasted_iota(jnp.int32, (PER_OWNER, PER_OWNER), 0)

    def second_turn(i, carry):
        source = columns.at[pl.ds(2 * i, 2)]
        for side in range(2):
            for k in range(WIDE // 128):
                turned[side, k * 128 : (k + 1) * 128, :] = source[side, :, k * 128 : (k + 1) * 128].T
        targets = [moved.at[pl.ds(high * 16 + 2 * i, 2)] for high in range(9)]
        for side in range(2):
            for high in range(8):
                order = order_ref[pl.ds(high * 16 + 2 * i + side, 1), :]
                chosen = jnp.where(pair == order, 1.0, 0.0).astype(jnp.bfloat16)
                values = turned[side, high * ROWS : (high + 1) * ROWS, :]
                placed[side, high * ROWS : (high + 1) * ROWS, :] = jnp.dot(
                    values, chosen, preferred_element_type=jnp.float32
                )
            for group in range(0, VALUES, 8):
                x = [placed[side, high * ROWS + group : high * ROWS + group + 8, :] for high in range(8)]
                for bit in range(3):
                    x = [jnp.where(moves[4 + bit], x[(high - (1 << bit)) % 8], x[high]) for high in range(8)]
                for high in range(9):
                    targets[high][side, group : group + 8, :] = x[(high - 1) % 8]
        return carry

    lax.fori_loop(0, 8, second_turn, 0, unroll=8)

    def leave(block):
        some = pl.ds(pl.multiple_of(block * LEAVE, LEAVE), LEAVE)
        return pltpu.make_async_copy(ready.at[some], out_hbm.at[some], out_sems.at[block])

    def finish(block, carry):
        source = moved.at[pl.ds(block * LEAVE + 1, LEAVE + 15)]
        target = ready.at[pl.ds(block * LEAVE, LEAVE)]
        for group in range(0, VALUES, 8):
            x = [source[i, group : group + 8, :] for i in range(LEAVE + 15)]
            for bit in reversed(range(4)):
                step = 1 << bit
                x = [jnp.where(moves[bit], x[i - step], x[i]) for i in range(step, len(x))]
            for i in range(LEAVE):
                target[i, group : group + 8, :] = x[i].astype(jnp.bfloat16)
        leave(block).start()
        return carry

    lax.fori_loop(0, DEVICES // LEAVE, finish, 0)
    for block in range(DEVICES // LEAVE):
        leave(block).wait()


def cross(order, shift, spectra):
    return pl.pallas_call(
        cross_kernel,
        out_shape=jax.ShapeDtypeStruct((DEVICES, VALUES, PER_OWNER), jnp.bfloat16),
        in_specs=[pl.BlockSpec(memory_space=pltpu.VMEM)] * 3,
        out_specs=pl.BlockSpec(memory_space=pltpu.HBM),
        scratch_shapes=[
            pltpu.VMEM((LANES_FULL // 128, 8 * SIXTEEN, 128), jnp.float32),
            pltpu.VMEM((STATIONS * APART, STATIONS), jnp.float32),
            pltpu.VMEM((16, STATIONS, WIDE), jnp.bfloat16),
            pltpu.VMEM((2, WIDE, STATIONS), jnp.bfloat16),
            pltpu.VMEM((2, WIDE, STATIONS), jnp.float32),
            pltpu.VMEM((DEVICES + 16, VALUES, PER_OWNER), jnp.float32),
            pltpu.VMEM((DEVICES, VALUES, PER_OWNER), jnp.bfloat16),
            pltpu.SemaphoreType.DMA((DEVICES // LEAVE,)),
        ],
        compiler_params=pltpu.CompilerParams(vmem_limit_bytes=28 * MIB),
    )(order, shift, spectra)


def lag_kernel(owner_ref, cross_ref, table_ref, place_ref, old_hbm, out_hbm, old, new, old_sems, new_sems):
    old_copies = [[pltpu.make_async_copy(old_hbm.at[c, d], old.at[c, d], old_sems.at[c, d]) for d in range(COMPONENTS)] for c in range(COMPONENTS)]
    for copy in sum(old_copies, []):
        copy.start()
    row = lax.broadcasted_iota(jnp.int32, (PER_OWNER, PER_OWNER), 0)
    chosen = jnp.where(row == place_ref[pl.ds(owner_ref[0], 1), :], 1.0, 0.0).astype(jnp.bfloat16)
    new_copies = []
    for c in range(COMPONENTS):
        rows = []
        for d in range(COMPONENTS):
            begin = (c * COMPONENTS + d) * PARTS
            spectra = cross_ref[:, begin : begin + PARTS, :].reshape(2 * FREQ_BINS, PER_OWNER)
            turned = lax.dot_general(chosen, spectra, NT, preferred_element_type=jnp.float32)
            rows.append(turned.astype(jnp.bfloat16))
        lagged = jnp.dot(jnp.concatenate(rows, axis=0), table_ref[...], preferred_element_type=jnp.float32)
        new[c] = lagged.reshape(COMPONENTS, PER_OWNER, LAG_BINS)
        for e in ((), (0, 1), (2,))[c]:
            for d in range(COMPONENTS):
                old_copies[e][d].wait()
                new[e, d] = old[e, d] + new[e, d]
                copy = pltpu.make_async_copy(new.at[e, d], out_hbm.at[e, d], new_sems.at[e, d])
                copy.start()
                new_copies.append(copy)
    for copy in new_copies:
        copy.wait()


def lag(owner, arrived, place, old_rows):
    return pl.pallas_call(
        lag_kernel,
        out_shape=jax.ShapeDtypeStruct(old_rows.shape, jnp.float32),
        in_specs=[pl.BlockSpec(memory_space=pltpu.SMEM)]
        + [pl.BlockSpec(memory_space=pltpu.VMEM)] * 3
        + [pl.BlockSpec(memory_space=pltpu.HBM)],
        out_specs=pl.BlockSpec(memory_space=pltpu.HBM),
        scratch_shapes=[
            pltpu.VMEM(old_rows.shape, jnp.float32),
            pltpu.VMEM(old_rows.shape, jnp.float32),
            pltpu.SemaphoreType.DMA((COMPONENTS, COMPONENTS)),
            pltpu.SemaphoreType.DMA((COMPONENTS, COMPONENTS)),
        ],
        compiler_params=pltpu.CompilerParams(vmem_limit_bytes=24 * MIB),
    )(owner, arrived, jnp.asarray(lag_table()), place, pltpu.with_memory_space_constraint(old_rows, pltpu.HBM))


def local(waveforms, availability, pair_slot, old_stack):
    axes = ("row", "col")
    spectra = whiten(waveforms.reshape(LANES, SAMPLES), availability)
    spectra = lax.all_to_all(spectra, axes, split_axis=0, concat_axis=0, tiled=True)
    order, place, shift = route(pair_slot)
    crossed = cross(order, shift, spectra)
    arrived = lax.all_to_all(crossed, axes, split_axis=0, concat_axis=0, tiled=True)
    old_rows = jnp.transpose(old_stack, (1, 2, 0, 3))
    owner = (lax.axis_index("row") * lax.axis_size("col") + lax.axis_index("col")).astype(jnp.int32).reshape(1)
    return jnp.transpose(lag(owner, arrived, place, old_rows), (2, 0, 1, 3))


def solution(mesh):
    return jax.shard_map(
        local,
        mesh=mesh,
        in_specs=(
            P(("row", "col"), None, None, None),
            P(("row", "col"), None),
            P(),
            P(("row", "col"), None, None, None),
        ),
        out_specs=P(("row", "col"), None, None, None),
        check_vma=False,
    )
```

```python
import math

import jax
import jax.numpy as jnp
import ml_dtypes
import numpy as np
from jax import lax
from jax.experimental import pallas as pl
from jax.experimental.pallas import tpu as pltpu
from jax.sharding import PartitionSpec as P

SEGMENTS = 160
COMPONENTS = 3
SAMPLES = 1024
LAG_BINS = 512
BAND_HALF = 64
FREQ_BINS = 512
DEVICES = 128
STATIONS = 128
PER_OWNER = 128
BINS = FREQ_BINS // DEVICES
PARTS = 2 * BINS
LANES = COMPONENTS * SEGMENTS
LANES_FULL = 512
PRODUCTS = COMPONENTS * COMPONENTS
VALUES = PRODUCTS * PARTS
ROWS = -(-VALUES // 16) * 16
APART = ROWS + 8
SIXTEEN = 16 * PARTS + 8
WIDE = 8 * ROWS

WHITEN_PIECES = 4
LEAVE = 32

EPSILON = 1e-06
MIB = 1024 * 1024
NT = (((1,), (1,)), ((), ()))
TN = (((0,), (0,)), ((), ()))


def bin_order():
    half = FREQ_BINS // 2
    return np.concatenate([np.arange(half + 1), np.arange(FREQ_BINS - 1, half, -1)])


def dft_table():
    half = FREQ_BINS // 2
    turns = np.arange(half + 1)[:, None] * np.arange(SAMPLES)[None, :] % SAMPLES
    turns = turns.astype(np.float32) * np.float32(2.0 * math.pi / SAMPLES)
    cosine, sine = np.cos(turns), -np.sin(turns)
    fill = np.zeros((14, SAMPLES), np.float32)
    table = np.concatenate([cosine[:half], sine[:half], cosine[half:], sine[half:], fill], axis=0)
    return table.astype(ml_dtypes.bfloat16)


def lag_table():
    bin_ids = bin_order()
    lag_ids = np.arange(LAG_BINS) - LAG_BINS // 2
    turns = bin_ids[:, None] * lag_ids[None, :] % SAMPLES
    turns = turns.astype(np.float32) * np.float32(2.0 * math.pi / SAMPLES)
    weight = np.where(bin_ids == 0, 1.0, 2.0).astype(np.float32)[:, None] / np.float32(math.sqrt(FREQ_BINS))
    both = np.stack([weight * np.cos(turns), -weight * np.sin(turns)])
    return both.transpose(1, 0, 2).reshape(2 * FREQ_BINS, LAG_BINS).astype(ml_dtypes.bfloat16)


def lane_runs():
    whole = [(c * SEGMENTS, c * 128, 128) for c in range(COMPONENTS)]
    rest = SEGMENTS - 128
    return whole + [(c * SEGMENTS + 128, COMPONENTS * 128 + c * rest, rest) for c in range(COMPONENTS)]


def whiten_kernel(
    avail_hbm, wave_hbm, dft_hbm, out_hbm, avail, wave, half_dft, dft, mixed, ready, avail_sem, wave_sems, dft_sems, out_sems
):
    half = FREQ_BINS // 2
    wave_copies = [
        pltpu.make_async_copy(wave_hbm.at[pl.ds(row, count)], wave.at[pl.ds(begin, count)], wave_sems.at[i])
        for i, (row, begin, count) in enumerate(lane_runs())
    ]
    dft_runs = [(p * half, half) for p in range(2)] + [(2 * half, 16)]
    dft_copies = [
        pltpu.make_async_copy(dft_hbm.at[pl.ds(row, count)], half_dft.at[pl.ds(row, count)], dft_sems.at[i])
        for i, (row, count) in enumerate(dft_runs)
    ]
    avail_copy = pltpu.make_async_copy(avail_hbm, avail, avail_sem)
    for copy in wave_copies + dft_copies + [avail_copy]:
        copy.start()
    wave[LANES:] = jnp.zeros((LANES_FULL - LANES, SAMPLES), jnp.bfloat16)

    def bin_of(row):
        return jnp.where(row <= half, row, 3 * half - row)

    square = (FREQ_BINS, FREQ_BINS)
    apart = bin_of(lax.broadcasted_iota(jnp.int32, square, 0)) - bin_of(lax.broadcasted_iota(jnp.int32, square, 1))
    near = jnp.where(jnp.abs(apart) <= BAND_HALF, 1.0, 0.0).astype(jnp.bfloat16)
    for copy in wave_copies:
        copy.wait()
    waves = wave[...].T
    odd = lax.broadcasted_iota(jnp.int32, (half, SAMPLES), 1) & 1 == 1
    top = lax.broadcasted_iota(jnp.int32, (half, SAMPLES), 0) == 0
    for copy in dft_copies:
        copy.wait()
    for p in range(2):
        lower = half_dft[p * half : (p + 1) * half]
        middle = half_dft[2 * half : 2 * half + 16][p : p + 1]
        mirrored = jnp.where(odd, -lower, lower) if p == 0 else jnp.where(odd, lower, -lower)
        dft[p * FREQ_BINS : p * FREQ_BINS + half] = lower
        dft[p * FREQ_BINS + half : (p + 1) * FREQ_BINS] = jnp.where(top, middle, mirrored)
    real = jnp.dot(dft[:FREQ_BINS], waves, preferred_element_type=jnp.float32)
    imag = jnp.dot(dft[FREQ_BINS:], waves, preferred_element_type=jnp.float32)
    power = real * real + imag * imag
    high = power.astype(jnp.bfloat16)
    low = (power - high.astype(jnp.float32)).astype(jnp.bfloat16)
    smooth = jnp.dot(near, high, preferred_element_type=jnp.float32) + jnp.dot(
        near, low, preferred_element_type=jnp.float32
    )
    bin_id = bin_of(lax.broadcasted_iota(jnp.int32, (FREQ_BINS, 1), 0))
    width = jnp.minimum(bin_id, BAND_HALF) + jnp.minimum(FREQ_BINS - 1 - bin_id, BAND_HALF) + 1
    lane = lax.broadcasted_iota(jnp.int32, (1, LANES_FULL), 1)
    segment = jnp.where(lane < COMPONENTS * 128, lane & 127, 128 + (lane & (SEGMENTS - 129)))
    avail_copy.wait()
    first, last = avail[0, 0], avail[0, 1]
    mask = ((segment >= first) & (segment < last) & (lane < LANES)).astype(jnp.float32)
    factor = lax.rsqrt(smooth * (1.0 / width.astype(jnp.float32)) + EPSILON) * mask
    spare = jnp.where(lane == LANES, first, jnp.where(lane == LANES + 1, last, 0)).astype(jnp.float32)
    out_copies = []
    bins = FREQ_BINS // WHITEN_PIECES
    for i in range(WHITEN_PIECES):
        rows = slice(i * bins, (i + 1) * bins)
        for p, values in enumerate((real[rows] * factor[rows] + spare, imag[rows] * factor[rows] + spare)):
            for t in range(LANES_FULL // 128):
                mixed[t, pl.ds(2 * i * bins + p, bins, stride=2), :] = values[:, t * 128 : (t + 1) * 128]
        some = pl.ds(i * bins // BINS, bins // BINS)
        for t in range(LANES_FULL // 128):
            values = mixed[t, 2 * i * bins : 2 * (i + 1) * bins, :].astype(jnp.bfloat16)
            ready[some, :, t * 128 : (t + 1) * 128] = values.reshape(bins // BINS, PARTS, 128)
        out_copies.append(pltpu.make_async_copy(ready.at[some], out_hbm.at[some], out_sems.at[i]))
        out_copies[i].start()
    for copy in out_copies:
        copy.wait()


def whiten(waves, availability):
    return pl.pallas_call(
        whiten_kernel,
        out_shape=pltpu.HBM((DEVICES, PARTS, LANES_FULL), jnp.bfloat16),
        in_specs=[pl.BlockSpec(memory_space=pltpu.HBM)] * 3,
        out_specs=pl.BlockSpec(memory_space=pltpu.HBM),
        scratch_shapes=[
            pltpu.SMEM((1, 2), jnp.int32),
            pltpu.VMEM((LANES_FULL, SAMPLES), jnp.bfloat16),
            pltpu.VMEM((FREQ_BINS + 16, SAMPLES), jnp.bfloat16),
            pltpu.VMEM((2 * FREQ_BINS, SAMPLES), jnp.bfloat16),
            pltpu.VMEM((LANES_FULL // 128, 2 * FREQ_BINS, 128), jnp.float32),
            pltpu.VMEM((DEVICES, PARTS, LANES_FULL), jnp.bfloat16),
            pltpu.SemaphoreType.DMA,
            pltpu.SemaphoreType.DMA((2 * COMPONENTS,)),
            pltpu.SemaphoreType.DMA((3,)),
            pltpu.SemaphoreType.DMA((WHITEN_PIECES,)),
        ],
        compiler_params=pltpu.CompilerParams(vmem_limit_bytes=24 * MIB),
    )(*(pltpu.with_memory_space_constraint(x, pltpu.HBM) for x in (availability, waves, jnp.asarray(dft_table()))))


def route_kernel(slot_ref, chosen_hbm, place_ref, shift_ref, order, chosen, chosen_sems):
    shape = (DEVICES, PER_OWNER)
    tile = lax.broadcasted_iota(jnp.int32, shape, 0)
    lane = lax.broadcasted_iota(jnp.int32, shape, 1)
    slots = slot_ref[...]
    shift = (slots // PER_OWNER - tile) & (DEVICES - 1)
    slot = slots & (PER_OWNER - 1)
    key = shift * PER_OWNER + lane

    def count(i, total):
        for k in range(8):
            total = total + (pltpu.roll(key, i * 8 + k, 1) < key).astype(jnp.int32)
        return total

    rank = lax.fori_loop(0, PER_OWNER // 8, count, jnp.zeros(shape, jnp.int32))
    packed = (rank << 21) | (shift << 14) | (lane << 7) | slot

    def pick(i, found):
        for k in range(8):
            turned = pltpu.roll(packed, i * 8 + k, 1)
            found = jnp.where((turned >> 21) == lane, turned, found)
        return found

    ordered = lax.fori_loop(0, PER_OWNER // 8, pick, jnp.zeros(shape, jnp.int32))
    order[...] = (ordered >> 7) & (PER_OWNER - 1)
    row = lax.broadcasted_iota(jnp.int32, shape, 0)

    def leave(block):
        some = pl.ds(block * 16, 16)
        return pltpu.make_async_copy(chosen.at[some], chosen_hbm.at[some], chosen_sems.at[block])

    def choose(block, carry):
        target, source = chosen.at[pl.ds(block * 16, 16)], order.at[pl.ds(pl.multiple_of(block * 16, 16), 16)]
        for i in range(16):
            target[i] = jnp.where(row == source[i : i + 1, :], 1.0, 0.0).astype(jnp.bfloat16)
        leave(block).start()
        return carry

    lax.fori_loop(0, 8, choose, 0)
    shift = (ordered >> 14) & (DEVICES - 1)
    shift_ref[...] = shift[:8]
    slot = ordered & (PER_OWNER - 1)
    for bit in range(7):
        slot = jnp.where((shift >> bit) & 1 == 1, pltpu.roll(slot, 1 << bit, 0), slot)
    place_ref[...] = slot
    for block in range(8):
        leave(block).wait()


def route(pair_slot):
    tiles = pair_slot.reshape(8, 16, 8, 16).transpose(0, 3, 1, 2).reshape(DEVICES, PER_OWNER)
    table = jax.ShapeDtypeStruct((DEVICES, PER_OWNER), jnp.int32)
    return pl.pallas_call(
        route_kernel,
        out_shape=(
            pltpu.HBM((DEVICES, PER_OWNER, PER_OWNER), jnp.bfloat16),
            table,
            jax.ShapeDtypeStruct((8, PER_OWNER), jnp.int32),
        ),
        in_specs=[pl.BlockSpec(memory_space=pltpu.VMEM)],
        out_specs=[pl.BlockSpec(memory_space=pltpu.HBM)] + [pl.BlockSpec(memory_space=pltpu.VMEM)] * 2,
        scratch_shapes=[
            pltpu.VMEM((DEVICES, PER_OWNER), jnp.int32),
            pltpu.VMEM((DEVICES, PER_OWNER, PER_OWNER), jnp.bfloat16),
            pltpu.SemaphoreType.DMA((8,)),
        ],
        compiler_params=pltpu.CompilerParams(vmem_limit_bytes=10 * MIB),
        cost_estimate=pl.CostEstimate(flops=40_000_000, bytes_accessed=200_000, transcendentals=0),
    )(tiles)


def cross_kernel(
    chosen_hbm,
    shift_ref,
    spec_ref,
    out_hbm,
    spec_full,
    planes,
    columns,
    turned,
    placed,
    moved,
    ready,
    chosen,
    chosen_sems,
    out_sems,
):
    chosen_copies = [
        pltpu.make_async_copy(chosen_hbm.at[pl.ds(i * 32, 32)], chosen.at[pl.ds(i * 32, 32)], chosen_sems.at[i])
        for i in range(4)
    ]
    for copy in chosen_copies:
        copy.start()
    wide = spec_ref[...].astype(jnp.float32).reshape(STATIONS * PARTS, LANES_FULL)
    tiles = LANES_FULL // 128
    for t in range(tiles):
        for high in range(8):
            rows = wide[high * 16 * PARTS : (high + 1) * 16 * PARTS, t * 128 : (t + 1) * 128]
            spec_full[t, high * SIXTEEN : high * SIXTEEN + 16 * PARTS] = rows

    def part(row, t):
        return jnp.concatenate(
            [spec_full[t, pl.ds(low * PARTS + row, 8, stride=SIXTEEN), :] for low in range(16)], axis=0
        )

    head = part(0, LANES // 128)
    spare = LANES % 128
    first = jnp.broadcast_to(head[:, spare : spare + 1], (STATIONS, STATIONS))
    last = jnp.broadcast_to(head[:, spare + 1 : spare + 2], (STATIONS, STATIONS))
    counts = jnp.minimum(last, last.T) - jnp.maximum(first, first.T)
    one = lax.broadcasted_iota(jnp.int32, (STATIONS, STATIONS), 0)
    two = lax.broadcasted_iota(jnp.int32, (STATIONS, STATIONS), 1)
    scale = jnp.where(one == two, 0.0, 1.0 / counts)

    def fold(row):
        pieces = [part(row, t).astype(jnp.bfloat16) for t in range(tiles)]
        rest = SEGMENTS - 128
        return jnp.concatenate(
            [
                jnp.concatenate([pieces[c], pieces[-1][:, c * rest : (c + 1) * rest]], axis=1)
                for c in range(COMPONENTS)
            ],
            axis=0,
        )

    def product(x, y):
        return jnp.dot(x, y, preferred_element_type=jnp.float32)

    for f in range(BINS):
        real, imag = fold(2 * f), fold(2 * f + 1)
        real_t, imag_t = real.T, imag.T
        stacked = jnp.concatenate([real, imag], axis=0)
        by_real, by_imag = product(stacked, real_t), product(stacked, imag_t)
        size = COMPONENTS * STATIONS
        both = (by_real[:size] + by_imag[size:], by_real[size:] - by_imag[:size])
        for p in range(2):
            for c in range(COMPONENTS):
                for d in range(COMPONENTS):
                    plane = both[p][c * STATIONS : (c + 1) * STATIONS, d * STATIONS : (d + 1) * STATIONS]
                    row = (c * COMPONENTS + d) * PARTS + 2 * f + p
                    planes[pl.ds(row, STATIONS, stride=APART), :] = plane * scale

    moves = [(shift_ref[...] >> bit) & 1 == 1 for bit in range(7)]

    def first_turn(i, carry):
        two = 16 * APART
        source = planes.at[pl.ds(pl.multiple_of(i * two, 8), two)]
        target = columns.at[:, pl.ds(pl.multiple_of(i * 16, 16), 16)]
        for k in range(WIDE // 128):
            sides = []
            for side in range(2):
                rows = []
                for begin in range(k * 128, (k + 1) * 128, 8):
                    high, value = divmod(begin, ROWS)
                    row = (side * 8 + high) * APART + value
                    rows.append(source[row : row + 8, :])
                rows = jnp.concatenate(rows, axis=0).astype(jnp.bfloat16).T
                sides.append(rows.astype(jnp.float32).reshape(16, 8, 128))
            target[:, :, k * 128 : (k + 1) * 128] = jnp.concatenate(sides, axis=1).astype(jnp.bfloat16)
        return carry

    lax.fori_loop(0, 8, first_turn, 0, unroll=8)

    for copy in chosen_copies:
        copy.wait()

    def second_turn(i, carry):
        source = columns.at[pl.ds(2 * i, 2)]
        for side in range(2):
            for k in range(WIDE // 128):
                turned[side, k * 128 : (k + 1) * 128, :] = source[side, :, k * 128 : (k + 1) * 128].T
        targets = [moved.at[pl.ds(high * 16 + 2 * i, 2)] for high in range(9)]
        for side in range(2):
            for high in range(8):
                values = turned[side, high * ROWS : (high + 1) * ROWS, :]
                placed[side, high * ROWS : (high + 1) * ROWS, :] = jnp.dot(
                    values, chosen[high * 16 + 2 * i + side], preferred_element_type=jnp.float32
                )
            for group in range(0, VALUES, 8):
                x = [placed[side, high * ROWS + group : high * ROWS + group + 8, :] for high in range(8)]
                for bit in range(3):
                    x = [jnp.where(moves[4 + bit], x[(high - (1 << bit)) % 8], x[high]) for high in range(8)]
                for high in range(9):
                    targets[high][side, group : group + 8, :] = x[(high - 1) % 8]
        return carry

    lax.fori_loop(0, 8, second_turn, 0, unroll=8)

    def leave(block):
        some = pl.ds(pl.multiple_of(block * LEAVE, LEAVE), LEAVE)
        return pltpu.make_async_copy(ready.at[some], out_hbm.at[some], out_sems.at[block])

    def finish(block, carry):
        source = moved.at[pl.ds(block * LEAVE + 1, LEAVE + 15)]
        target = ready.at[pl.ds(block * LEAVE, LEAVE)]
        for group in range(0, VALUES, 8):
            x = [source[i, group : group + 8, :] for i in range(LEAVE + 15)]
            for bit in reversed(range(4)):
                step = 1 << bit
                x = [jnp.where(moves[bit], x[i - step], x[i]) for i in range(step, len(x))]
            for i in range(LEAVE):
                target[i, group : group + 8, :] = x[i].astype(jnp.bfloat16)
        leave(block).start()
        return carry

    lax.fori_loop(0, DEVICES // LEAVE, finish, 0)
    for block in range(DEVICES // LEAVE):
        leave(block).wait()


def cross(chosen, shift, spectra):
    return pl.pallas_call(
        cross_kernel,
        out_shape=pltpu.HBM((DEVICES, VALUES, PER_OWNER), jnp.bfloat16),
        in_specs=[pl.BlockSpec(memory_space=pltpu.HBM)] + [pl.BlockSpec(memory_space=pltpu.VMEM)] * 2,
        out_specs=pl.BlockSpec(memory_space=pltpu.HBM),
        scratch_shapes=[
            pltpu.VMEM((LANES_FULL // 128, 8 * SIXTEEN, 128), jnp.float32),
            pltpu.VMEM((STATIONS * APART, STATIONS), jnp.float32),
            pltpu.VMEM((16, STATIONS, WIDE), jnp.bfloat16),
            pltpu.VMEM((2, WIDE, STATIONS), jnp.bfloat16),
            pltpu.VMEM((2, WIDE, STATIONS), jnp.float32),
            pltpu.VMEM((DEVICES + 16, VALUES, PER_OWNER), jnp.float32),
            pltpu.VMEM((DEVICES, VALUES, PER_OWNER), jnp.bfloat16),
            pltpu.VMEM((DEVICES, PER_OWNER, PER_OWNER), jnp.bfloat16),
            pltpu.SemaphoreType.DMA((4,)),
            pltpu.SemaphoreType.DMA((DEVICES // LEAVE,)),
        ],
        compiler_params=pltpu.CompilerParams(vmem_limit_bytes=32 * MIB),
    )(pltpu.with_memory_space_constraint(chosen, pltpu.HBM), shift, spectra)


def lag_kernel(owner_ref, cross_ref, table_ref, place_ref, old_hbm, out_hbm, old, new, old_sems, new_sems):
    old_copies = [[pltpu.make_async_copy(old_hbm.at[c, d], old.at[c, d], old_sems.at[c, d]) for d in range(COMPONENTS)] for c in range(COMPONENTS)]
    for copy in sum(old_copies, []):
        copy.start()
    row = lax.broadcasted_iota(jnp.int32, (PER_OWNER, PER_OWNER), 0)
    chosen = jnp.where(row == place_ref[pl.ds(owner_ref[0], 1), :], 1.0, 0.0).astype(jnp.bfloat16)
    new_copies = []
    for c in range(COMPONENTS):
        rows = []
        for d in range(COMPONENTS):
            begin = (c * COMPONENTS + d) * PARTS
            spectra = cross_ref[:, begin : begin + PARTS, :].reshape(2 * FREQ_BINS, PER_OWNER)
            turned = lax.dot_general(chosen, spectra, NT, preferred_element_type=jnp.float32)
            rows.append(turned.astype(jnp.bfloat16))
        lagged = jnp.dot(jnp.concatenate(rows, axis=0), table_ref[...], preferred_element_type=jnp.float32)
        new[c] = lagged.reshape(COMPONENTS, PER_OWNER, LAG_BINS)
        for e in ((), (0, 1), (2,))[c]:
            for d in range(COMPONENTS):
                old_copies[e][d].wait()
                new[e, d] = old[e, d] + new[e, d]
                copy = pltpu.make_async_copy(new.at[e, d], out_hbm.at[e, d], new_sems.at[e, d])
                copy.start()
                new_copies.append(copy)
    for copy in new_copies:
        copy.wait()


def lag(owner, arrived, place, old_rows):
    return pl.pallas_call(
        lag_kernel,
        out_shape=pltpu.HBM(old_rows.shape, jnp.float32),
        in_specs=[pl.BlockSpec(memory_space=pltpu.SMEM)]
        + [pl.BlockSpec(memory_space=pltpu.VMEM)] * 3
        + [pl.BlockSpec(memory_space=pltpu.HBM)],
        out_specs=pl.BlockSpec(memory_space=pltpu.HBM),
        scratch_shapes=[
            pltpu.VMEM(old_rows.shape, jnp.float32),
            pltpu.VMEM(old_rows.shape, jnp.float32),
            pltpu.SemaphoreType.DMA((COMPONENTS, COMPONENTS)),
            pltpu.SemaphoreType.DMA((COMPONENTS, COMPONENTS)),
        ],
        compiler_params=pltpu.CompilerParams(vmem_limit_bytes=24 * MIB),
    )(owner, arrived, jnp.asarray(lag_table()), place, pltpu.with_memory_space_constraint(old_rows, pltpu.HBM))


def local(waveforms, availability, pair_slot, old_stack):
    axes = ("row", "col")
    spectra = whiten(waveforms.reshape(LANES, SAMPLES), availability)
    spectra = lax.all_to_all(spectra, axes, split_axis=0, concat_axis=0, tiled=True)
    chosen, place, shift = route(pair_slot)
    crossed = cross(chosen, shift, spectra)
    arrived = lax.all_to_all(crossed, axes, split_axis=0, concat_axis=0, tiled=True)
    old_rows = jnp.transpose(old_stack, (1, 2, 0, 3))
    owner = (lax.axis_index("row") * lax.axis_size("col") + lax.axis_index("col")).astype(jnp.int32).reshape(1)
    return jnp.transpose(lag(owner, arrived, place, old_rows), (2, 0, 1, 3))


def solution(mesh):
    return jax.shard_map(
        local,
        mesh=mesh,
        in_specs=(
            P(("row", "col"), None, None, None),
            P(("row", "col"), None),
            P(),
            P(("row", "col"), None, None, None),
        ),
        out_specs=P(("row", "col"), None, None, None),
        check_vma=False,
    )
```

```python
import math

import jax
import jax.numpy as jnp
import ml_dtypes
import numpy as np
from jax import lax
from jax.experimental import pallas as pl
from jax.experimental.pallas import tpu as pltpu
from jax.sharding import PartitionSpec as P

SEGMENTS = 160
COMPONENTS = 3
SAMPLES = 1024
LAG_BINS = 512
BAND_HALF = 64
FREQ_BINS = 512
DEVICES = 128
STATIONS = 128
PER_OWNER = 128
BINS = FREQ_BINS // DEVICES
PARTS = 2 * BINS
LANES = COMPONENTS * SEGMENTS
LANES_FULL = 512
PRODUCTS = COMPONENTS * COMPONENTS
VALUES = PRODUCTS * PARTS
ROWS = -(-VALUES // 16) * 16
APART = ROWS + 8
SIXTEEN = 16 * PARTS + 8
WIDE = 8 * ROWS

WHITEN_PIECES = 4
LEAVE = 32

EPSILON = 1e-06
MIB = 1024 * 1024
NT = (((1,), (1,)), ((), ()))
TN = (((0,), (0,)), ((), ()))


def bin_order():
    half = FREQ_BINS // 2
    return np.concatenate([np.arange(half + 1), np.arange(FREQ_BINS - 1, half, -1)])


def dft_table():
    half = FREQ_BINS // 2
    turns = np.arange(half + 1)[:, None] * np.arange(SAMPLES)[None, :] % SAMPLES
    turns = turns.astype(np.float32) * np.float32(2.0 * math.pi / SAMPLES)
    cosine, sine = np.cos(turns), -np.sin(turns)
    fill = np.zeros((14, SAMPLES), np.float32)
    table = np.concatenate([cosine[:half], sine[:half], cosine[half:], sine[half:], fill], axis=0)
    return table.astype(ml_dtypes.bfloat16)


def lag_table():
    bin_ids = bin_order()
    lag_ids = np.arange(LAG_BINS) - LAG_BINS // 2
    turns = bin_ids[:, None] * lag_ids[None, :] % SAMPLES
    turns = turns.astype(np.float32) * np.float32(2.0 * math.pi / SAMPLES)
    weight = np.where(bin_ids == 0, 1.0, 2.0).astype(np.float32)[:, None] / np.float32(math.sqrt(FREQ_BINS))
    both = np.stack([weight * np.cos(turns), -weight * np.sin(turns)])
    return both.transpose(1, 0, 2).reshape(2 * FREQ_BINS, LAG_BINS).astype(ml_dtypes.bfloat16)


def lane_runs():
    whole = [(c * SEGMENTS, c * 128, 128) for c in range(COMPONENTS)]
    rest = SEGMENTS - 128
    return whole + [(c * SEGMENTS + 128, COMPONENTS * 128 + c * rest, rest) for c in range(COMPONENTS)]


def whiten_kernel(
    avail_hbm, wave_hbm, dft_hbm, out_hbm, avail, wave, half_dft, dft, mixed, ready, avail_sem, wave_sems, dft_sems, out_sems
):
    half = FREQ_BINS // 2
    wave_copies = [
        pltpu.make_async_copy(wave_hbm.at[pl.ds(row, count)], wave.at[pl.ds(begin, count)], wave_sems.at[i])
        for i, (row, begin, count) in enumerate(lane_runs())
    ]
    dft_runs = [(p * half, half) for p in range(2)] + [(2 * half, 16)]
    dft_copies = [
        pltpu.make_async_copy(dft_hbm.at[pl.ds(row, count)], half_dft.at[pl.ds(row, count)], dft_sems.at[i])
        for i, (row, count) in enumerate(dft_runs)
    ]
    avail_copy = pltpu.make_async_copy(avail_hbm, avail, avail_sem)
    for copy in wave_copies + dft_copies + [avail_copy]:
        copy.start()
    wave[LANES:] = jnp.zeros((LANES_FULL - LANES, SAMPLES), jnp.bfloat16)

    def bin_of(row):
        return jnp.where(row <= half, row, 3 * half - row)

    square = (FREQ_BINS, FREQ_BINS)
    apart = bin_of(lax.broadcasted_iota(jnp.int32, square, 0)) - bin_of(lax.broadcasted_iota(jnp.int32, square, 1))
    near = jnp.where(jnp.abs(apart) <= BAND_HALF, 1.0, 0.0).astype(jnp.bfloat16)
    for copy in wave_copies:
        copy.wait()
    waves = wave[...].T
    odd = lax.broadcasted_iota(jnp.int32, (half, SAMPLES), 1) & 1 == 1
    top = lax.broadcasted_iota(jnp.int32, (half, SAMPLES), 0) == 0
    for copy in dft_copies:
        copy.wait()
    for p in range(2):
        lower = half_dft[p * half : (p + 1) * half]
        middle = half_dft[2 * half : 2 * half + 16][p : p + 1]
        mirrored = jnp.where(odd, -lower, lower) if p == 0 else jnp.where(odd, lower, -lower)
        dft[p * FREQ_BINS : p * FREQ_BINS + half] = lower
        dft[p * FREQ_BINS + half : (p + 1) * FREQ_BINS] = jnp.where(top, middle, mirrored)
    real = jnp.dot(dft[:FREQ_BINS], waves, preferred_element_type=jnp.float32)
    imag = jnp.dot(dft[FREQ_BINS:], waves, preferred_element_type=jnp.float32)
    power = real * real + imag * imag
    high = power.astype(jnp.bfloat16)
    low = (power - high.astype(jnp.float32)).astype(jnp.bfloat16)
    smooth = jnp.dot(near, high, preferred_element_type=jnp.float32) + jnp.dot(
        near, low, preferred_element_type=jnp.float32
    )
    bin_id = bin_of(lax.broadcasted_iota(jnp.int32, (FREQ_BINS, 1), 0))
    width = jnp.minimum(bin_id, BAND_HALF) + jnp.minimum(FREQ_BINS - 1 - bin_id, BAND_HALF) + 1
    lane = lax.broadcasted_iota(jnp.int32, (1, LANES_FULL), 1)
    segment = jnp.where(lane < COMPONENTS * 128, lane & 127, 128 + (lane & (SEGMENTS - 129)))
    avail_copy.wait()
    first, last = avail[0, 0], avail[0, 1]
    mask = ((segment >= first) & (segment < last) & (lane < LANES)).astype(jnp.float32)
    factor = lax.rsqrt(smooth * (1.0 / width.astype(jnp.float32)) + EPSILON) * mask
    spare = jnp.where(lane == LANES, first, jnp.where(lane == LANES + 1, last, 0)).astype(jnp.float32)
    out_copies = []
    bins = FREQ_BINS // WHITEN_PIECES
    for i in range(WHITEN_PIECES):
        rows = slice(i * bins, (i + 1) * bins)
        for p, values in enumerate((real[rows] * factor[rows] + spare, imag[rows] * factor[rows] + spare)):
            for t in range(LANES_FULL // 128):
                mixed[t, pl.ds(2 * i * bins + p, bins, stride=2), :] = values[:, t * 128 : (t + 1) * 128]
        some = pl.ds(i * bins // BINS, bins // BINS)
        for t in range(LANES_FULL // 128):
            values = mixed[t, 2 * i * bins : 2 * (i + 1) * bins, :].astype(jnp.bfloat16)
            ready[some, :, t * 128 : (t + 1) * 128] = values.reshape(bins // BINS, PARTS, 128)
        out_copies.append(pltpu.make_async_copy(ready.at[some], out_hbm.at[some], out_sems.at[i]))
        out_copies[i].start()
    for copy in out_copies:
        copy.wait()


def whiten(waves, availability):
    return pl.pallas_call(
        whiten_kernel,
        out_shape=pltpu.HBM((DEVICES, PARTS, LANES_FULL), jnp.bfloat16),
        in_specs=[pl.BlockSpec(memory_space=pltpu.HBM)] * 3,
        out_specs=pl.BlockSpec(memory_space=pltpu.HBM),
        scratch_shapes=[
            pltpu.SMEM((1, 2), jnp.int32),
            pltpu.VMEM((LANES_FULL, SAMPLES), jnp.bfloat16),
            pltpu.VMEM((FREQ_BINS + 16, SAMPLES), jnp.bfloat16),
            pltpu.VMEM((2 * FREQ_BINS, SAMPLES), jnp.bfloat16),
            pltpu.VMEM((LANES_FULL // 128, 2 * FREQ_BINS, 128), jnp.float32),
            pltpu.VMEM((DEVICES, PARTS, LANES_FULL), jnp.bfloat16),
            pltpu.SemaphoreType.DMA,
            pltpu.SemaphoreType.DMA((2 * COMPONENTS,)),
            pltpu.SemaphoreType.DMA((3,)),
            pltpu.SemaphoreType.DMA((WHITEN_PIECES,)),
        ],
        compiler_params=pltpu.CompilerParams(vmem_limit_bytes=24 * MIB),
    )(*(pltpu.with_memory_space_constraint(x, pltpu.HBM) for x in (availability, waves, jnp.asarray(dft_table()))))


def route_kernel(slot_ref, chosen_hbm, place_ref, shift_ref, order, chosen, chosen_sems):
    shape = (DEVICES, PER_OWNER)
    tile = lax.broadcasted_iota(jnp.int32, shape, 0)
    lane = lax.broadcasted_iota(jnp.int32, shape, 1)
    slots = slot_ref[...]
    shift = (slots // PER_OWNER - tile) & (DEVICES - 1)
    slot = slots & (PER_OWNER - 1)
    key = shift * PER_OWNER + lane

    def count(i, total):
        for k in range(8):
            total = total + (pltpu.roll(key, i * 8 + k, 1) < key).astype(jnp.int32)
        return total

    rank = lax.fori_loop(0, PER_OWNER // 8, count, jnp.zeros(shape, jnp.int32))
    packed = (rank << 21) | (shift << 14) | (lane << 7) | slot

    def pick(i, found):
        for k in range(8):
            turned = pltpu.roll(packed, i * 8 + k, 1)
            found = jnp.where((turned >> 21) == lane, turned, found)
        return found

    ordered = lax.fori_loop(0, PER_OWNER // 8, pick, jnp.zeros(shape, jnp.int32))
    order[...] = (ordered >> 7) & (PER_OWNER - 1)
    row = lax.broadcasted_iota(jnp.int32, shape, 0)

    def leave(block):
        some = pl.ds(block * 16, 16)
        return pltpu.make_async_copy(chosen.at[some], chosen_hbm.at[some], chosen_sems.at[block])

    def choose(block, carry):
        target, source = chosen.at[pl.ds(block * 16, 16)], order.at[pl.ds(pl.multiple_of(block * 16, 16), 16)]
        for i in range(16):
            target[i] = jnp.where(row == source[i : i + 1, :], 1.0, 0.0).astype(jnp.bfloat16)
        leave(block).start()
        return carry

    lax.fori_loop(0, 8, choose, 0)
    shift = (ordered >> 14) & (DEVICES - 1)
    shift_ref[...] = shift[:8]
    slot = ordered & (PER_OWNER - 1)
    for bit in range(7):
        slot = jnp.where((shift >> bit) & 1 == 1, pltpu.roll(slot, 1 << bit, 0), slot)
    place_ref[...] = slot
    for block in range(8):
        leave(block).wait()


def route(pair_slot):
    tiles = pair_slot.reshape(8, 16, 8, 16).transpose(0, 3, 1, 2).reshape(DEVICES, PER_OWNER)
    table = jax.ShapeDtypeStruct((DEVICES, PER_OWNER), jnp.int32)
    return pl.pallas_call(
        route_kernel,
        out_shape=(
            pltpu.HBM((DEVICES, PER_OWNER, PER_OWNER), jnp.bfloat16),
            table,
            jax.ShapeDtypeStruct((8, PER_OWNER), jnp.int32),
        ),
        in_specs=[pl.BlockSpec(memory_space=pltpu.VMEM)],
        out_specs=[pl.BlockSpec(memory_space=pltpu.HBM)] + [pl.BlockSpec(memory_space=pltpu.VMEM)] * 2,
        scratch_shapes=[
            pltpu.VMEM((DEVICES, PER_OWNER), jnp.int32),
            pltpu.VMEM((DEVICES, PER_OWNER, PER_OWNER), jnp.bfloat16),
            pltpu.SemaphoreType.DMA((8,)),
        ],
        compiler_params=pltpu.CompilerParams(vmem_limit_bytes=10 * MIB),
        cost_estimate=pl.CostEstimate(flops=40_000_000, bytes_accessed=200_000, transcendentals=0),
    )(tiles)


def cross_kernel(
    chosen_hbm,
    shift_ref,
    spec_ref,
    out_hbm,
    spec_full,
    planes,
    columns,
    turned,
    placed,
    moved,
    ready,
    chosen,
    chosen_sems,
    out_sems,
):
    chosen_copies = [
        pltpu.make_async_copy(chosen_hbm.at[pl.ds(i * 32, 32)], chosen.at[pl.ds(i * 32, 32)], chosen_sems.at[i])
        for i in range(4)
    ]
    for copy in chosen_copies:
        copy.start()
    wide = spec_ref[...].astype(jnp.float32).reshape(STATIONS * PARTS, LANES_FULL)
    tiles = LANES_FULL // 128
    for t in range(tiles):
        for high in range(8):
            rows = wide[high * 16 * PARTS : (high + 1) * 16 * PARTS, t * 128 : (t + 1) * 128]
            spec_full[t, high * SIXTEEN : high * SIXTEEN + 16 * PARTS] = rows

    def part(row, t):
        return jnp.concatenate(
            [spec_full[t, pl.ds(low * PARTS + row, 8, stride=SIXTEEN), :] for low in range(16)], axis=0
        )

    head = part(0, LANES // 128)
    spare = LANES % 128
    first = jnp.broadcast_to(head[:, spare : spare + 1], (STATIONS, STATIONS))
    last = jnp.broadcast_to(head[:, spare + 1 : spare + 2], (STATIONS, STATIONS))
    counts = jnp.minimum(last, last.T) - jnp.maximum(first, first.T)
    one = lax.broadcasted_iota(jnp.int32, (STATIONS, STATIONS), 0)
    two = lax.broadcasted_iota(jnp.int32, (STATIONS, STATIONS), 1)
    scale = jnp.where(one == two, 0.0, 1.0 / counts)

    def fold(row):
        pieces = [part(row, t).astype(jnp.bfloat16) for t in range(tiles)]
        rest = SEGMENTS - 128
        return jnp.concatenate(
            [
                jnp.concatenate([pieces[c], pieces[-1][:, c * rest : (c + 1) * rest]], axis=1)
                for c in range(COMPONENTS)
            ],
            axis=0,
        )

    def product(x, y):
        return jnp.dot(x, y, preferred_element_type=jnp.float32)

    folded = [(fold(2 * f), fold(2 * f + 1)) for f in range(BINS)]
    folded_t = [(real.T, imag.T) for real, imag in folded]

    def multiply(begin, count):
        for f in range(BINS):
            stacked = jnp.concatenate(
                [
                    side[c * STATIONS + begin : c * STATIONS + begin + count]
                    for side in folded[f]
                    for c in range(COMPONENTS)
                ],
                axis=0,
            )
            by_real, by_imag = product(stacked, folded_t[f][0]), product(stacked, folded_t[f][1])
            size = COMPONENTS * count
            both = (by_real[:size] + by_imag[size:], by_real[size:] - by_imag[:size])
            for p in range(2):
                for c in range(COMPONENTS):
                    for d in range(COMPONENTS):
                        plane = both[p][c * count : (c + 1) * count, d * STATIONS : (d + 1) * STATIONS]
                        row = (c * COMPONENTS + d) * PARTS + 2 * f + p
                        planes[pl.ds(begin * APART + row, count, stride=APART), :] = plane * scale[begin : begin + count]

    moves = [(shift_ref[...] >> bit) & 1 == 1 for bit in range(7)]

    def first_turn(i):
        two = 16 * APART
        source = planes.at[pl.ds(i * two, two)]
        target = columns.at[:, pl.ds(i * 16, 16)]
        for k in range(WIDE // 128):
            sides = []
            for side in range(2):
                rows = []
                for begin in range(k * 128, (k + 1) * 128, 8):
                    high, value = divmod(begin, ROWS)
                    row = (side * 8 + high) * APART + value
                    rows.append(source[row : row + 8, :])
                rows = jnp.concatenate(rows, axis=0).astype(jnp.bfloat16).T
                sides.append(rows.astype(jnp.float32).reshape(16, 8, 128))
            target[:, :, k * 128 : (k + 1) * 128] = jnp.concatenate(sides, axis=1).astype(jnp.bfloat16)

    for block in range(2):
        multiply(block * STATIONS // 2, STATIONS // 2)
        for i in range(4 * block, 4 * block + 4):
            first_turn(i)

    for copy in chosen_copies:
        copy.wait()

    def second_turn(i, carry):
        source = columns.at[pl.ds(2 * i, 2)]
        for side in range(2):
            for k in range(WIDE // 128):
                turned[side, k * 128 : (k + 1) * 128, :] = source[side, :, k * 128 : (k + 1) * 128].T
        targets = [moved.at[pl.ds(high * 16 + 2 * i, 2)] for high in range(9)]
        for side in range(2):
            for high in range(8):
                values = turned[side, high * ROWS : (high + 1) * ROWS, :]
                placed[side, high * ROWS : (high + 1) * ROWS, :] = jnp.dot(
                    values, chosen[high * 16 + 2 * i + side], preferred_element_type=jnp.float32
                )
            for group in range(0, VALUES, 8):
                x = [placed[side, high * ROWS + group : high * ROWS + group + 8, :] for high in range(8)]
                for bit in range(3):
                    x = [jnp.where(moves[4 + bit], x[(high - (1 << bit)) % 8], x[high]) for high in range(8)]
                for high in range(9):
                    targets[high][side, group : group + 8, :] = x[(high - 1) % 8]
        return carry

    lax.fori_loop(0, 8, second_turn, 0, unroll=8)

    def leave(block):
        some = pl.ds(pl.multiple_of(block * LEAVE, LEAVE), LEAVE)
        return pltpu.make_async_copy(ready.at[some], out_hbm.at[some], out_sems.at[block])

    def finish(block, carry):
        source = moved.at[pl.ds(block * LEAVE + 1, LEAVE + 15)]
        target = ready.at[pl.ds(block * LEAVE, LEAVE)]
        for group in range(0, VALUES, 8):
            x = [source[i, group : group + 8, :] for i in range(LEAVE + 15)]
            for bit in reversed(range(4)):
                step = 1 << bit
                x = [jnp.where(moves[bit], x[i - step], x[i]) for i in range(step, len(x))]
            for i in range(LEAVE):
                target[i, group : group + 8, :] = x[i].astype(jnp.bfloat16)
        leave(block).start()
        return carry

    lax.fori_loop(0, DEVICES // LEAVE, finish, 0)
    for block in range(DEVICES // LEAVE):
        leave(block).wait()


def cross(chosen, shift, spectra):
    return pl.pallas_call(
        cross_kernel,
        out_shape=pltpu.HBM((DEVICES, VALUES, PER_OWNER), jnp.bfloat16),
        in_specs=[pl.BlockSpec(memory_space=pltpu.HBM)] + [pl.BlockSpec(memory_space=pltpu.VMEM)] * 2,
        out_specs=pl.BlockSpec(memory_space=pltpu.HBM),
        scratch_shapes=[
            pltpu.VMEM((LANES_FULL // 128, 8 * SIXTEEN, 128), jnp.float32),
            pltpu.VMEM((STATIONS * APART, STATIONS), jnp.float32),
            pltpu.VMEM((16, STATIONS, WIDE), jnp.bfloat16),
            pltpu.VMEM((2, WIDE, STATIONS), jnp.bfloat16),
            pltpu.VMEM((2, WIDE, STATIONS), jnp.float32),
            pltpu.VMEM((DEVICES + 16, VALUES, PER_OWNER), jnp.float32),
            pltpu.VMEM((DEVICES, VALUES, PER_OWNER), jnp.bfloat16),
            pltpu.VMEM((DEVICES, PER_OWNER, PER_OWNER), jnp.bfloat16),
            pltpu.SemaphoreType.DMA((4,)),
            pltpu.SemaphoreType.DMA((DEVICES // LEAVE,)),
        ],
        compiler_params=pltpu.CompilerParams(vmem_limit_bytes=32 * MIB),
    )(pltpu.with_memory_space_constraint(chosen, pltpu.HBM), shift, spectra)


def lag_kernel(owner_ref, cross_ref, table_ref, place_ref, old_hbm, out_hbm, old, new, old_sems, new_sems):
    old_copies = [[pltpu.make_async_copy(old_hbm.at[c, d], old.at[c, d], old_sems.at[c, d]) for d in range(COMPONENTS)] for c in range(COMPONENTS)]
    for copy in sum(old_copies, []):
        copy.start()
    row = lax.broadcasted_iota(jnp.int32, (PER_OWNER, PER_OWNER), 0)
    chosen = jnp.where(row == place_ref[pl.ds(owner_ref[0], 1), :], 1.0, 0.0).astype(jnp.bfloat16)
    new_copies = []
    for c in range(COMPONENTS):
        rows = []
        for d in range(COMPONENTS):
            begin = (c * COMPONENTS + d) * PARTS
            spectra = cross_ref[:, begin : begin + PARTS, :].reshape(2 * FREQ_BINS, PER_OWNER)
            turned = lax.dot_general(chosen, spectra, NT, preferred_element_type=jnp.float32)
            rows.append(turned.astype(jnp.bfloat16))
        lagged = jnp.dot(jnp.concatenate(rows, axis=0), table_ref[...], preferred_element_type=jnp.float32)
        new[c] = lagged.reshape(COMPONENTS, PER_OWNER, LAG_BINS)
        for e in ((), (0, 1), (2,))[c]:
            for d in range(COMPONENTS):
                old_copies[e][d].wait()
                new[e, d] = old[e, d] + new[e, d]
                copy = pltpu.make_async_copy(new.at[e, d], out_hbm.at[e, d], new_sems.at[e, d])
                copy.start()
                new_copies.append(copy)
    for copy in new_copies:
        copy.wait()


def lag(owner, arrived, place, old_rows):
    return pl.pallas_call(
        lag_kernel,
        out_shape=pltpu.HBM(old_rows.shape, jnp.float32),
        in_specs=[pl.BlockSpec(memory_space=pltpu.SMEM)]
        + [pl.BlockSpec(memory_space=pltpu.VMEM)] * 3
        + [pl.BlockSpec(memory_space=pltpu.HBM)],
        out_specs=pl.BlockSpec(memory_space=pltpu.HBM),
        scratch_shapes=[
            pltpu.VMEM(old_rows.shape, jnp.float32),
            pltpu.VMEM(old_rows.shape, jnp.float32),
            pltpu.SemaphoreType.DMA((COMPONENTS, COMPONENTS)),
            pltpu.SemaphoreType.DMA((COMPONENTS, COMPONENTS)),
        ],
        compiler_params=pltpu.CompilerParams(vmem_limit_bytes=24 * MIB),
    )(owner, arrived, jnp.asarray(lag_table()), place, pltpu.with_memory_space_constraint(old_rows, pltpu.HBM))


def local(waveforms, availability, pair_slot, old_stack):
    axes = ("row", "col")
    spectra = whiten(waveforms.reshape(LANES, SAMPLES), availability)
    spectra = lax.all_to_all(spectra, axes, split_axis=0, concat_axis=0, tiled=True)
    chosen, place, shift = route(pair_slot)
    crossed = cross(chosen, shift, spectra)
    arrived = lax.all_to_all(crossed, axes, split_axis=0, concat_axis=0, tiled=True)
    old_rows = jnp.transpose(old_stack, (1, 2, 0, 3))
    owner = (lax.axis_index("row") * lax.axis_size("col") + lax.axis_index("col")).astype(jnp.int32).reshape(1)
    return jnp.transpose(lag(owner, arrived, place, old_rows), (2, 0, 1, 3))


def solution(mesh):
    return jax.shard_map(
        local,
        mesh=mesh,
        in_specs=(
            P(("row", "col"), None, None, None),
            P(("row", "col"), None),
            P(),
            P(("row", "col"), None, None, None),
        ),
        out_specs=P(("row", "col"), None, None, None),
        check_vma=False,
    )
```

```python
import math

import jax
import jax.numpy as jnp
import ml_dtypes
import numpy as np
from jax import lax
from jax.experimental import pallas as pl
from jax.experimental.pallas import tpu as pltpu
from jax.sharding import PartitionSpec as P

SEGMENTS = 160
COMPONENTS = 3
SAMPLES = 1024
LAG_BINS = 512
BAND_HALF = 64
FREQ_BINS = 512
DEVICES = 128
STATIONS = 128
PER_OWNER = 128
BINS = FREQ_BINS // DEVICES
PARTS = 2 * BINS
LANES = COMPONENTS * SEGMENTS
LANES_FULL = 512
PRODUCTS = COMPONENTS * COMPONENTS
VALUES = PRODUCTS * PARTS
ROWS = -(-VALUES // 16) * 16
APART = ROWS + 8
SIXTEEN = 16 * PARTS + 8
WIDE = 8 * ROWS

WHITEN_PIECES = 4
LEAVE = 32

EPSILON = 1e-06
MIB = 1024 * 1024
NT = (((1,), (1,)), ((), ()))
TN = (((0,), (0,)), ((), ()))


def bin_order():
    half = FREQ_BINS // 2
    return np.concatenate([np.arange(half + 1), np.arange(FREQ_BINS - 1, half, -1)])


def dft_table():
    half = FREQ_BINS // 2
    turns = np.arange(half + 1)[:, None] * np.arange(SAMPLES)[None, :] % SAMPLES
    turns = turns.astype(np.float32) * np.float32(2.0 * math.pi / SAMPLES)
    cosine, sine = np.cos(turns), -np.sin(turns)
    fill = np.zeros((14, SAMPLES), np.float32)
    table = np.concatenate([cosine[:half], sine[:half], cosine[half:], sine[half:], fill], axis=0)
    return table.astype(ml_dtypes.bfloat16)


def lag_table():
    bin_ids = bin_order()
    lag_ids = np.arange(LAG_BINS) - LAG_BINS // 2
    turns = bin_ids[:, None] * lag_ids[None, :] % SAMPLES
    turns = turns.astype(np.float32) * np.float32(2.0 * math.pi / SAMPLES)
    weight = np.where(bin_ids == 0, 1.0, 2.0).astype(np.float32)[:, None] / np.float32(math.sqrt(FREQ_BINS))
    both = np.stack([weight * np.cos(turns), -weight * np.sin(turns)])
    return both.transpose(1, 0, 2).reshape(2 * FREQ_BINS, LAG_BINS).astype(ml_dtypes.bfloat16)


def lane_runs():
    whole = [(c * SEGMENTS, c * 128, 128) for c in range(COMPONENTS)]
    rest = SEGMENTS - 128
    return whole + [(c * SEGMENTS + 128, COMPONENTS * 128 + c * rest, rest) for c in range(COMPONENTS)]


def whiten_kernel(
    avail_hbm, wave_hbm, dft_hbm, out_hbm, avail, wave, half_dft, dft, mixed, ready, avail_sem, wave_sems, dft_sems, out_sems
):
    half = FREQ_BINS // 2
    wave_copies = [
        pltpu.make_async_copy(wave_hbm.at[pl.ds(row, count)], wave.at[pl.ds(begin, count)], wave_sems.at[i])
        for i, (row, begin, count) in enumerate(lane_runs())
    ]
    dft_runs = [(p * half, half) for p in range(2)] + [(2 * half, 16)]
    dft_copies = [
        pltpu.make_async_copy(dft_hbm.at[pl.ds(row, count)], half_dft.at[pl.ds(row, count)], dft_sems.at[i])
        for i, (row, count) in enumerate(dft_runs)
    ]
    avail_copy = pltpu.make_async_copy(avail_hbm, avail, avail_sem)
    for copy in wave_copies + dft_copies + [avail_copy]:
        copy.start()
    wave[LANES:] = jnp.zeros((LANES_FULL - LANES, SAMPLES), jnp.bfloat16)

    def bin_of(row):
        return jnp.where(row <= half, row, 3 * half - row)

    square = (FREQ_BINS, FREQ_BINS)
    apart = bin_of(lax.broadcasted_iota(jnp.int32, square, 0)) - bin_of(lax.broadcasted_iota(jnp.int32, square, 1))
    near = jnp.where(jnp.abs(apart) <= BAND_HALF, 1.0, 0.0).astype(jnp.bfloat16)
    for copy in wave_copies:
        copy.wait()
    waves = wave[...].T
    odd = lax.broadcasted_iota(jnp.int32, (half, SAMPLES), 1) & 1 == 1
    top = lax.broadcasted_iota(jnp.int32, (half, SAMPLES), 0) == 0
    for copy in dft_copies:
        copy.wait()
    for p in range(2):
        lower = half_dft[p * half : (p + 1) * half]
        middle = half_dft[2 * half : 2 * half + 16][p : p + 1]
        mirrored = jnp.where(odd, -lower, lower) if p == 0 else jnp.where(odd, lower, -lower)
        dft[p * FREQ_BINS : p * FREQ_BINS + half] = lower
        dft[p * FREQ_BINS + half : (p + 1) * FREQ_BINS] = jnp.where(top, middle, mirrored)
    real = jnp.dot(dft[:FREQ_BINS], waves, preferred_element_type=jnp.float32)
    imag = jnp.dot(dft[FREQ_BINS:], waves, preferred_element_type=jnp.float32)
    power = real * real + imag * imag
    high = power.astype(jnp.bfloat16)
    low = (power - high.astype(jnp.float32)).astype(jnp.bfloat16)
    smooth = jnp.dot(
        jnp.concatenate([near, near], axis=1),
        jnp.concatenate([high, low], axis=0),
        preferred_element_type=jnp.float32,
    )
    bin_id = bin_of(lax.broadcasted_iota(jnp.int32, (FREQ_BINS, 1), 0))
    width = jnp.minimum(bin_id, BAND_HALF) + jnp.minimum(FREQ_BINS - 1 - bin_id, BAND_HALF) + 1
    lane = lax.broadcasted_iota(jnp.int32, (1, LANES_FULL), 1)
    segment = jnp.where(lane < COMPONENTS * 128, lane & 127, 128 + (lane & (SEGMENTS - 129)))
    avail_copy.wait()
    first, last = avail[0, 0], avail[0, 1]
    mask = ((segment >= first) & (segment < last) & (lane < LANES)).astype(jnp.float32)
    factor = lax.rsqrt(smooth * (1.0 / width.astype(jnp.float32)) + EPSILON) * mask
    spare = jnp.where(lane == LANES, first, jnp.where(lane == LANES + 1, last, 0)).astype(jnp.float32)
    out_copies = []
    bins = FREQ_BINS // WHITEN_PIECES
    for i in range(WHITEN_PIECES):
        rows = slice(i * bins, (i + 1) * bins)
        for p, values in enumerate((real[rows] * factor[rows] + spare, imag[rows] * factor[rows] + spare)):
            for t in range(LANES_FULL // 128):
                mixed[t, pl.ds(2 * i * bins + p, bins, stride=2), :] = values[:, t * 128 : (t + 1) * 128]
        some = pl.ds(i * bins // BINS, bins // BINS)
        for t in range(LANES_FULL // 128):
            values = mixed[t, 2 * i * bins : 2 * (i + 1) * bins, :].astype(jnp.bfloat16)
            ready[some, :, t * 128 : (t + 1) * 128] = values.reshape(bins // BINS, PARTS, 128)
        out_copies.append(pltpu.make_async_copy(ready.at[some], out_hbm.at[some], out_sems.at[i]))
        out_copies[i].start()
    for copy in out_copies:
        copy.wait()


def whiten(waves, availability):
    return pl.pallas_call(
        whiten_kernel,
        out_shape=pltpu.HBM((DEVICES, PARTS, LANES_FULL), jnp.bfloat16),
        in_specs=[pl.BlockSpec(memory_space=pltpu.HBM)] * 3,
        out_specs=pl.BlockSpec(memory_space=pltpu.HBM),
        scratch_shapes=[
            pltpu.SMEM((1, 2), jnp.int32),
            pltpu.VMEM((LANES_FULL, SAMPLES), jnp.bfloat16),
            pltpu.VMEM((FREQ_BINS + 16, SAMPLES), jnp.bfloat16),
            pltpu.VMEM((2 * FREQ_BINS, SAMPLES), jnp.bfloat16),
            pltpu.VMEM((LANES_FULL // 128, 2 * FREQ_BINS, 128), jnp.float32),
            pltpu.VMEM((DEVICES, PARTS, LANES_FULL), jnp.bfloat16),
            pltpu.SemaphoreType.DMA,
            pltpu.SemaphoreType.DMA((2 * COMPONENTS,)),
            pltpu.SemaphoreType.DMA((3,)),
            pltpu.SemaphoreType.DMA((WHITEN_PIECES,)),
        ],
        compiler_params=pltpu.CompilerParams(vmem_limit_bytes=24 * MIB),
    )(*(pltpu.with_memory_space_constraint(x, pltpu.HBM) for x in (availability, waves, jnp.asarray(dft_table()))))


def route_kernel(slot_ref, chosen_hbm, place_ref, shift_ref, order, chosen, chosen_sems):
    shape = (DEVICES, PER_OWNER)
    tile = lax.broadcasted_iota(jnp.int32, shape, 0)
    lane = lax.broadcasted_iota(jnp.int32, shape, 1)
    slots = slot_ref[...]
    shift = (slots // PER_OWNER - tile) & (DEVICES - 1)
    slot = slots & (PER_OWNER - 1)
    key = shift * PER_OWNER + lane

    def count(i, total):
        for k in range(8):
            total = total + (pltpu.roll(key, i * 8 + k, 1) < key).astype(jnp.int32)
        return total

    rank = lax.fori_loop(0, PER_OWNER // 8, count, jnp.zeros(shape, jnp.int32))
    packed = (rank << 21) | (shift << 14) | (lane << 7) | slot

    def pick(i, found):
        for k in range(8):
            turned = pltpu.roll(packed, i * 8 + k, 1)
            found = jnp.where((turned >> 21) == lane, turned, found)
        return found

    ordered = lax.fori_loop(0, PER_OWNER // 8, pick, jnp.zeros(shape, jnp.int32))
    order[...] = (ordered >> 7) & (PER_OWNER - 1)
    row = lax.broadcasted_iota(jnp.int32, shape, 0)

    def leave(block):
        some = pl.ds(block * 16, 16)
        return pltpu.make_async_copy(chosen.at[some], chosen_hbm.at[some], chosen_sems.at[block])

    def choose(block, carry):
        target, source = chosen.at[pl.ds(block * 16, 16)], order.at[pl.ds(pl.multiple_of(block * 16, 16), 16)]
        for i in range(16):
            target[i] = jnp.where(row == source[i : i + 1, :], 1.0, 0.0).astype(jnp.bfloat16)
        leave(block).start()
        return carry

    lax.fori_loop(0, 8, choose, 0)
    shift = (ordered >> 14) & (DEVICES - 1)
    shift_ref[...] = shift[:8]
    slot = ordered & (PER_OWNER - 1)
    for bit in range(7):
        slot = jnp.where((shift >> bit) & 1 == 1, pltpu.roll(slot, 1 << bit, 0), slot)
    place_ref[...] = slot
    for block in range(8):
        leave(block).wait()


def route(pair_slot):
    tiles = pair_slot.reshape(8, 16, 8, 16).transpose(0, 3, 1, 2).reshape(DEVICES, PER_OWNER)
    table = jax.ShapeDtypeStruct((DEVICES, PER_OWNER), jnp.int32)
    return pl.pallas_call(
        route_kernel,
        out_shape=(
            pltpu.HBM((DEVICES, PER_OWNER, PER_OWNER), jnp.bfloat16),
            table,
            jax.ShapeDtypeStruct((8, PER_OWNER), jnp.int32),
        ),
        in_specs=[pl.BlockSpec(memory_space=pltpu.VMEM)],
        out_specs=[pl.BlockSpec(memory_space=pltpu.HBM)] + [pl.BlockSpec(memory_space=pltpu.VMEM)] * 2,
        scratch_shapes=[
            pltpu.VMEM((DEVICES, PER_OWNER), jnp.int32),
            pltpu.VMEM((DEVICES, PER_OWNER, PER_OWNER), jnp.bfloat16),
            pltpu.SemaphoreType.DMA((8,)),
        ],
        compiler_params=pltpu.CompilerParams(vmem_limit_bytes=10 * MIB),
        cost_estimate=pl.CostEstimate(flops=40_000_000, bytes_accessed=200_000, transcendentals=0),
    )(tiles)


def cross_kernel(
    chosen_hbm,
    shift_ref,
    spec_ref,
    out_hbm,
    spec_full,
    planes,
    columns,
    turned,
    placed,
    moved,
    ready,
    chosen,
    chosen_sems,
    out_sems,
):
    chosen_copies = [
        pltpu.make_async_copy(chosen_hbm.at[pl.ds(i * 32, 32)], chosen.at[pl.ds(i * 32, 32)], chosen_sems.at[i])
        for i in range(4)
    ]
    for copy in chosen_copies:
        copy.start()
    wide = spec_ref[...].astype(jnp.float32).reshape(STATIONS * PARTS, LANES_FULL)
    tiles = LANES_FULL // 128
    for t in range(tiles):
        for high in range(8):
            rows = wide[high * 16 * PARTS : (high + 1) * 16 * PARTS, t * 128 : (t + 1) * 128]
            spec_full[t, high * SIXTEEN : high * SIXTEEN + 16 * PARTS] = rows

    def part(row, t):
        return jnp.concatenate(
            [spec_full[t, pl.ds(low * PARTS + row, 8, stride=SIXTEEN), :] for low in range(16)], axis=0
        )

    head = part(0, LANES // 128)
    spare = LANES % 128
    first = jnp.broadcast_to(head[:, spare : spare + 1], (STATIONS, STATIONS))
    last = jnp.broadcast_to(head[:, spare + 1 : spare + 2], (STATIONS, STATIONS))
    counts = jnp.minimum(last, last.T) - jnp.maximum(first, first.T)
    one = lax.broadcasted_iota(jnp.int32, (STATIONS, STATIONS), 0)
    two = lax.broadcasted_iota(jnp.int32, (STATIONS, STATIONS), 1)
    scale = jnp.where(one == two, 0.0, 1.0 / counts)

    def fold(row):
        pieces = [part(row, t).astype(jnp.bfloat16) for t in range(tiles)]
        rest = SEGMENTS - 128
        return jnp.concatenate(
            [
                jnp.concatenate([pieces[c], pieces[-1][:, c * rest : (c + 1) * rest]], axis=1)
                for c in range(COMPONENTS)
            ],
            axis=0,
        )

    def product(x, y):
        return jnp.dot(x, y, preferred_element_type=jnp.float32)

    folded = [(fold(2 * f), fold(2 * f + 1)) for f in range(BINS)]
    folded_t = [(real.T, imag.T) for real, imag in folded]

    def multiply(begin, count):
        for f in range(BINS):
            stacked = jnp.concatenate(
                [
                    side[c * STATIONS + begin : c * STATIONS + begin + count]
                    for side in folded[f]
                    for c in range(COMPONENTS)
                ],
                axis=0,
            )
            by_real, by_imag = product(stacked, folded_t[f][0]), product(stacked, folded_t[f][1])
            size = COMPONENTS * count
            both = (by_real[:size] + by_imag[size:], by_real[size:] - by_imag[:size])
            for p in range(2):
                for c in range(COMPONENTS):
                    for d in range(COMPONENTS):
                        plane = both[p][c * count : (c + 1) * count, d * STATIONS : (d + 1) * STATIONS]
                        row = (c * COMPONENTS + d) * PARTS + 2 * f + p
                        planes[pl.ds(begin * APART + row, count, stride=APART), :] = plane * scale[begin : begin + count]

    moves = [(shift_ref[...] >> bit) & 1 == 1 for bit in range(7)]

    def first_turn(i):
        two = 16 * APART
        source = planes.at[pl.ds(i * two, two)]
        target = columns.at[:, pl.ds(i * 16, 16)]
        for k in range(WIDE // 128):
            sides = []
            for side in range(2):
                rows = []
                for begin in range(k * 128, (k + 1) * 128, 8):
                    high, value = divmod(begin, ROWS)
                    row = (side * 8 + high) * APART + value
                    rows.append(source[row : row + 8, :])
                rows = jnp.concatenate(rows, axis=0).astype(jnp.bfloat16).T
                sides.append(rows.astype(jnp.float32).reshape(16, 8, 128))
            target[:, :, k * 128 : (k + 1) * 128] = jnp.concatenate(sides, axis=1).astype(jnp.bfloat16)

    for block in range(2):
        multiply(block * STATIONS // 2, STATIONS // 2)
        for i in range(4 * block, 4 * block + 4):
            first_turn(i)

    for copy in chosen_copies:
        copy.wait()

    def second_turn(i, carry):
        source = columns.at[pl.ds(2 * i, 2)]
        for side in range(2):
            for k in range(WIDE // 128):
                turned[side, k * 128 : (k + 1) * 128, :] = source[side, :, k * 128 : (k + 1) * 128].T
        targets = [moved.at[pl.ds(high * 16 + 2 * i, 2)] for high in range(9)]
        for side in range(2):
            for high in range(8):
                values = turned[side, high * ROWS : (high + 1) * ROWS, :]
                placed[side, high * ROWS : (high + 1) * ROWS, :] = jnp.dot(
                    values, chosen[high * 16 + 2 * i + side], preferred_element_type=jnp.float32
                )
            for group in range(0, VALUES, 8):
                x = [placed[side, high * ROWS + group : high * ROWS + group + 8, :] for high in range(8)]
                for bit in range(3):
                    x = [jnp.where(moves[4 + bit], x[(high - (1 << bit)) % 8], x[high]) for high in range(8)]
                for high in range(9):
                    targets[high][side, group : group + 8, :] = x[(high - 1) % 8]
        return carry

    lax.fori_loop(0, 8, second_turn, 0, unroll=8)

    def leave(block):
        some = pl.ds(pl.multiple_of(block * LEAVE, LEAVE), LEAVE)
        return pltpu.make_async_copy(ready.at[some], out_hbm.at[some], out_sems.at[block])

    def finish(block, carry):
        source = moved.at[pl.ds(block * LEAVE + 1, LEAVE + 15)]
        target = ready.at[pl.ds(block * LEAVE, LEAVE)]
        for group in range(0, VALUES, 8):
            x = [source[i, group : group + 8, :] for i in range(LEAVE + 15)]
            for bit in reversed(range(4)):
                step = 1 << bit
                x = [jnp.where(moves[bit], x[i - step], x[i]) for i in range(step, len(x))]
            for i in range(LEAVE):
                target[i, group : group + 8, :] = x[i].astype(jnp.bfloat16)
        leave(block).start()
        return carry

    lax.fori_loop(0, DEVICES // LEAVE, finish, 0)
    for block in range(DEVICES // LEAVE):
        leave(block).wait()


def cross(chosen, shift, spectra):
    return pl.pallas_call(
        cross_kernel,
        out_shape=pltpu.HBM((DEVICES, VALUES, PER_OWNER), jnp.bfloat16),
        in_specs=[pl.BlockSpec(memory_space=pltpu.HBM)] + [pl.BlockSpec(memory_space=pltpu.VMEM)] * 2,
        out_specs=pl.BlockSpec(memory_space=pltpu.HBM),
        scratch_shapes=[
            pltpu.VMEM((LANES_FULL // 128, 8 * SIXTEEN, 128), jnp.float32),
            pltpu.VMEM((STATIONS * APART, STATIONS), jnp.float32),
            pltpu.VMEM((16, STATIONS, WIDE), jnp.bfloat16),
            pltpu.VMEM((2, WIDE, STATIONS), jnp.bfloat16),
            pltpu.VMEM((2, WIDE, STATIONS), jnp.float32),
            pltpu.VMEM((DEVICES + 16, VALUES, PER_OWNER), jnp.float32),
            pltpu.VMEM((DEVICES, VALUES, PER_OWNER), jnp.bfloat16),
            pltpu.VMEM((DEVICES, PER_OWNER, PER_OWNER), jnp.bfloat16),
            pltpu.SemaphoreType.DMA((4,)),
            pltpu.SemaphoreType.DMA((DEVICES // LEAVE,)),
        ],
        compiler_params=pltpu.CompilerParams(vmem_limit_bytes=32 * MIB),
    )(pltpu.with_memory_space_constraint(chosen, pltpu.HBM), shift, spectra)


def lag_kernel(owner_ref, cross_ref, table_ref, place_ref, old_hbm, out_hbm, old, new, old_sems, new_sems):
    old_copies = [[pltpu.make_async_copy(old_hbm.at[c, d], old.at[c, d], old_sems.at[c, d]) for d in range(COMPONENTS)] for c in range(COMPONENTS)]
    for copy in sum(old_copies, []):
        copy.start()
    row = lax.broadcasted_iota(jnp.int32, (PER_OWNER, PER_OWNER), 0)
    chosen = jnp.where(row == place_ref[pl.ds(owner_ref[0], 1), :], 1.0, 0.0).astype(jnp.bfloat16)
    new_copies = []
    def turn(c):
        rows = []
        for d in range(COMPONENTS):
            begin = (c * COMPONENTS + d) * PARTS
            spectra = cross_ref[:, begin : begin + PARTS, :].reshape(2 * FREQ_BINS, PER_OWNER)
            turned = lax.dot_general(chosen, spectra, NT, preferred_element_type=jnp.float32)
            rows.append(turned.astype(jnp.bfloat16))
        return jnp.concatenate(rows, axis=0)

    ahead = turn(0)
    for c in range(COMPONENTS):
        rows = ahead
        if c + 1 < COMPONENTS:
            ahead = turn(c + 1)
        lagged = jnp.dot(rows, table_ref[...], preferred_element_type=jnp.float32)
        new[c] = lagged.reshape(COMPONENTS, PER_OWNER, LAG_BINS)
        for e in ((), (0, 1), (2,))[c]:
            for d in range(COMPONENTS):
                old_copies[e][d].wait()
                new[e, d] = old[e, d] + new[e, d]
                copy = pltpu.make_async_copy(new.at[e, d], out_hbm.at[e, d], new_sems.at[e, d])
                copy.start()
                new_copies.append(copy)
    for copy in new_copies:
        copy.wait()


def lag(owner, arrived, place, old_rows):
    return pl.pallas_call(
        lag_kernel,
        out_shape=pltpu.HBM(old_rows.shape, jnp.float32),
        in_specs=[pl.BlockSpec(memory_space=pltpu.SMEM)]
        + [pl.BlockSpec(memory_space=pltpu.VMEM)] * 3
        + [pl.BlockSpec(memory_space=pltpu.HBM)],
        out_specs=pl.BlockSpec(memory_space=pltpu.HBM),
        scratch_shapes=[
            pltpu.VMEM(old_rows.shape, jnp.float32),
            pltpu.VMEM(old_rows.shape, jnp.float32),
            pltpu.SemaphoreType.DMA((COMPONENTS, COMPONENTS)),
            pltpu.SemaphoreType.DMA((COMPONENTS, COMPONENTS)),
        ],
        compiler_params=pltpu.CompilerParams(vmem_limit_bytes=24 * MIB),
    )(owner, arrived, jnp.asarray(lag_table()), place, pltpu.with_memory_space_constraint(old_rows, pltpu.HBM))


def local(waveforms, availability, pair_slot, old_stack):
    axes = ("row", "col")
    spectra = whiten(waveforms.reshape(LANES, SAMPLES), availability)
    spectra = lax.all_to_all(spectra, axes, split_axis=0, concat_axis=0, tiled=True)
    chosen, place, shift = route(pair_slot)
    crossed = cross(chosen, shift, spectra)
    arrived = lax.all_to_all(crossed, axes, split_axis=0, concat_axis=0, tiled=True)
    old_rows = jnp.transpose(old_stack, (1, 2, 0, 3))
    owner = (lax.axis_index("row") * lax.axis_size("col") + lax.axis_index("col")).astype(jnp.int32).reshape(1)
    return jnp.transpose(lag(owner, arrived, place, old_rows), (2, 0, 1, 3))


def solution(mesh):
    return jax.shard_map(
        local,
        mesh=mesh,
        in_specs=(
            P(("row", "col"), None, None, None),
            P(("row", "col"), None),
            P(),
            P(("row", "col"), None, None, None),
        ),
        out_specs=P(("row", "col"), None, None, None),
        check_vma=False,
    )
```
